768 devices in a mesh: blk: 48 (over z, x_lo, core), dp: 16 (over y, x_hi).
Axes of the slice: x: 4 (x_hi: 2, x_lo: 2; x = x_hi * 2 + x_lo), y: 8, z: 12, core: 2. Of those that a mesh axis runs over, the one named last changes fastest.
Arguments:
- tokens: bfloat16 [6144, 3072], P('dp'), may hold values from -6 to 6
- cotangent: bfloat16 [6144, 3072], P('dp'), may hold values from -0.59765625 to 0.59765625
- w_gate: bfloat16 [3072, 18432], P(None, 'blk'), may hold values from -0.109375 to 0.109375
- w_up: bfloat16 [3072, 18432], P(None, 'blk'), may hold values from -0.109375 to 0.109375
- w_down_t: bfloat16 [3072, 18432], P(None, 'blk'), may hold values from -0.046875 to 0.046875
- gate_probs: float32 [6144, 2], P('dp'), may hold values from 0.1 to 0.9
- slot_ids: int32 [6144], P('dp'), may hold values from 0 to 1
- block_list: int32 [16, 2], P('dp'), may hold values from 0 to 2, as said below
- block_count: int32 [16], P('dp'), may hold values from 1 to 2, as said below
Outputs:
- grad_tokens: bfloat16 [6144, 3072], P('dp', 'blk')
- grad_probs: float32 [6144, 2], P('dp')
- grad_gate: bfloat16 [3072, 18432], P('dp', 'blk')
- grad_up: bfloat16 [3072, 18432], P('dp', 'blk')
- grad_down_t: bfloat16 [3072, 18432], P('dp', 'blk')
The draws below stay inside these ranges and needn't reach their ends.
Inputs may be any that keep to these rules, and one draw needn't show every extreme that they name: `block_list`: each row holds 2 different block numbers of the group. `block_count`: in every draw some group has 2 live blocks and another group one.
All inputs are finite; a program needn't handle non-finite values.
Results may differ from the reference program's by a relative error of at most 0.019.
Values may be sent and summed in bfloat16 or wider, within the bound.
A program may use at most 64 MiB of HBM per device.

```python
import jax
import jax.numpy as jnp
from jax import lax

D = 3072
BLOCK = 128
BLOCKS_DEV = 3
NB_MAX = 2
FF = 18432
TOK_DEV = 384
TOKENS = 6144
N_DP = 16


def draw_block_list(key, part):
    key = jax.random.fold_in(key, 11)
    keys = jax.random.split(key, N_DP)
    orders = jax.vmap(lambda single: jax.random.permutation(single, BLOCKS_DEV))(keys)
    return orders[:, :NB_MAX].astype(jnp.int32)


def draw_block_count(key, part):
    key = jax.random.fold_in(key, 23)
    first, second = jax.random.split(key)
    counts = jax.random.randint(first, (N_DP,), 1, NB_MAX + 1).astype(jnp.int32)
    chosen = jax.random.randint(second, (), 0, N_DP).astype(jnp.int32)
    counts = counts.at[chosen].set(NB_MAX)
    counts = counts.at[(chosen + 1) % N_DP].set(1)
    return counts


def touch_ends(result, own_key, least, high):
    spot = [jax.random.randint(jax.random.fold_in(own_key, axis), (), 0, length) for axis, length in enumerate(result.shape)]
    main_axis = result.shape.index(max(result.shape))
    next_to = spot[:main_axis] + [(spot[main_axis] + 1) % result.shape[main_axis]] + spot[main_axis + 1:]
    return result.at[tuple(spot)].set(least).at[tuple(next_to)].set(high)


def with_spikes(values, own_key, source, target, blocks, factor):
    owner, partner = [(jnp.arange(values.shape[dim]) // (values.shape[dim] // blocks)).reshape([-1 if axis == dim else 1 for axis in range(values.ndim)]) for dim in (source, target)]
    chosen = jax.random.permutation(own_key, blocks)[partner]
    strong = (owner == chosen) | (owner == (partner + blocks // 2) % blocks)
    return jnp.where(strong, factor * values, values)


def block_levels(stream_key, dims, cuts, low, largest):
    factor_of = 1.0
    for axis_at, parts in cuts:
        heights = jax.random.uniform(jax.random.fold_in(jax.random.fold_in(stream_key, 6), axis_at), (parts,), jnp.float32, low / len(cuts), largest / len(cuts))
        factor_of = factor_of * jnp.repeat(jnp.exp(heights), dims[axis_at] // parts).reshape((-1,) + (1,) * (len(dims) - 1 - axis_at))
    return factor_of


def noise(own_key, shape, deviation, bound, shards=(), kind=jnp.bfloat16):
    drawn = jax.random.normal(own_key, shape, jnp.float32) * deviation
    if len(shards) > 0:
        drawn = block_levels(own_key, shape, shards, -0.22, 0.18) * drawn
    return jnp.clip(drawn, min=-bound, max=bound).astype(kind)


def bell_draw_with(rng, shape, width, limit, shards, heavy, dtype=jnp.bfloat16):
    entries = width * jax.random.normal(rng, shape, jnp.float32)
    if shards:
        entries = entries * block_levels(rng, shape, shards, -0.22, 0.18)
    return jnp.clip(with_spikes(entries, jax.random.fold_in(rng, 3), *heavy), -limit, limit).astype(dtype)


def setup_inputs(seed: int = 0) -> dict:
    splits = jax.random.split(jax.random.key(seed), 10)
    tokens = bell_draw_with(splits[0], (TOKENS, D), 1.0, 6.0, ((0, 16),), (0, 1, 16, 2.0))
    cotangent = noise(splits[1], (TOKENS, D), 0.1, 0.59765625, ((0, 16),))
    w_gate = noise(splits[2], (D, FF), D ** -0.5, 0.109375, ((1, 48),))
    w_up = noise(splits[3], (D, FF), D ** -0.5, 0.109375, ((1, 48),))
    w_down_t = noise(splits[4], (D, FF), FF ** -0.5, 0.046875, ((1, 48),))
    gate_probs = jnp.clip(0.1 + 0.79999997 * jax.random.uniform(splits[5], (TOKENS, 2), jnp.float32) ** block_levels(splits[5], (TOKENS, 2), ((0, 16),), -0.2, 0.2), 0.1, 0.9)
    slot_ids = touch_ends(jax.random.randint(splits[6], (TOKENS,), 0, 2), jax.random.fold_in(splits[6], 1), 0, 1).astype(jnp.int32)
    block_list = draw_block_list(jax.random.fold_in(splits[9], 71), 0)
    block_count = draw_block_count(jax.random.fold_in(splits[9], 71), 0)
    return dict(tokens=tokens, cotangent=cotangent, w_gate=w_gate, w_up=w_up, w_down_t=w_down_t, gate_probs=gate_probs, slot_ids=slot_ids, block_list=block_list, block_count=block_count)


def group_rows(source, blocks):
    pieces = []
    for which in range(NB_MAX):
        offset = (blocks[which] * BLOCK).astype(jnp.int32)
        pieces.append(lax.dynamic_slice_in_dim(source, offset, BLOCK, 0))
    return jnp.concatenate(pieces, axis=0)


def reference(tokens, cotangent, w_gate, w_up, w_down_t, gate_probs, slot_ids, block_list, block_count):
    grad_tokens = jnp.zeros((TOKENS, D), jnp.bfloat16)
    grad_probs = jnp.zeros((TOKENS, 2), jnp.float32)
    sums_gate = jnp.zeros((D, FF), jnp.float32)
    sums_up = jnp.zeros((D, FF), jnp.float32)
    sums_down = jnp.zeros((D, FF), jnp.float32)
    for group in range(N_DP):
        base = group * TOK_DEV
        blocks = block_list[group]
        filled = block_count[group]
        rows_in = group_rows(tokens[base:base + TOK_DEV], blocks)
        rows_cot = group_rows(cotangent[base:base + TOK_DEV], blocks)
        probs = group_rows(gate_probs[base:base + TOK_DEV], blocks)
        slots = group_rows(slot_ids[base:base + TOK_DEV], blocks)
        live = jnp.concatenate([jnp.full((BLOCK,), 1.0, jnp.float32) * (which < filled).astype(jnp.float32) for which in range(NB_MAX)])
        gates = jnp.where(slots == 0, probs[:, 0], probs[:, 1])
        pre_gate = jnp.dot(rows_in, w_gate, preferred_element_type=jnp.float32)
        pre_up = jnp.dot(rows_in, w_up, preferred_element_type=jnp.float32)
        sigmoid_gate = jax.nn.sigmoid(pre_gate)
        activated = pre_gate * sigmoid_gate
        hidden = (activated * pre_up).astype(jnp.bfloat16)
        back = jnp.dot(rows_cot, w_down_t, preferred_element_type=jnp.float32)
        dots = jnp.sum(hidden.astype(jnp.float32) * back, axis=1)
        values = dots * live
        columns = jnp.stack([jnp.where(slots == 0, values, 0.0), jnp.where(slots == 1, values, 0.0)], axis=1)
        factor = (gates * live)[:, None]
        d_hidden = back * factor
        d_pre_gate = (d_hidden * pre_up * sigmoid_gate * (1.0 + pre_gate * (1.0 - sigmoid_gate))).astype(jnp.bfloat16)
        d_pre_up = (d_hidden * activated).astype(jnp.bfloat16)
        scaled_hidden = (hidden.astype(jnp.float32) * factor).astype(jnp.bfloat16)
        rows_grad = (jnp.dot(d_pre_gate, w_gate.T, preferred_element_type=jnp.float32) + jnp.dot(d_pre_up, w_up.T, preferred_element_type=jnp.float32)).astype(jnp.bfloat16)
        for which in range(NB_MAX):
            offset = (base + blocks[which] * BLOCK).astype(jnp.int32)
            grad_tokens = lax.dynamic_update_slice_in_dim(grad_tokens, rows_grad[which * BLOCK:(which + 1) * BLOCK], offset, 0)
            grad_probs = lax.dynamic_update_slice_in_dim(grad_probs, columns[which * BLOCK:(which + 1) * BLOCK], offset, 0)
        part_gate = lax.optimization_barrier(jnp.dot(rows_in.T, d_pre_gate, preferred_element_type=jnp.float32).astype(jnp.bfloat16))
        part_up = lax.optimization_barrier(jnp.dot(rows_in.T, d_pre_up, preferred_element_type=jnp.float32).astype(jnp.bfloat16))
        part_down = lax.optimization_barrier(jnp.dot(rows_cot.T, scaled_hidden, preferred_element_type=jnp.float32).astype(jnp.bfloat16))
        sums_gate = sums_gate + part_gate.astype(jnp.float32)
        sums_up = sums_up + part_up.astype(jnp.float32)
        sums_down = sums_down + part_down.astype(jnp.float32)
    return (grad_tokens, grad_probs, sums_gate.astype(jnp.bfloat16), sums_up.astype(jnp.bfloat16), sums_down.astype(jnp.bfloat16))
```

```python
import jax
import jax.numpy as jnp
from jax import lax
from jax.experimental import pallas as pl
from jax.experimental.pallas import tpu as pltpu
from jax.sharding import PartitionSpec as P

MESH = pl.DeviceIdType.MESH
BF = jnp.bfloat16
F32 = jnp.float32

D = 3072
HID = 384
BLOCK = 128
TOK = 384
ROWS = 256
NY = 8
NZ = 12
SHARD = 192
FEAT = 64
CHUNK = 384

DOWN, UP = 0, 1
HOPS = {(0, DOWN): 4, (0, UP): 3, (1, DOWN): 3, (1, UP): 4, (2, DOWN): 4, (2, UP): 3, (3, DOWN): 3, (3, UP): 4}


def dot_lead(left, right):
    return lax.dot_general(left, right, (((0,), (0,)), ((), ())), preferred_element_type=F32)


def dot_last(left, right):
    return lax.dot_general(left, right, (((1,), (1,)), ((), ())), preferred_element_type=F32)


def kernel(
    list_ref, count_ref, probs_ref, slots_ref, tok_hbm, cot_hbm, wg_hbm, wu_hbm, wd_hbm,
    gtok_out, gprob_out, gg_out, gu_out, gd_out,
    tok, cot, wg, wu, wd, rin, rct, f_gate, f_up, f_back, hid, scaled, dpre, fac, picks,
    p_down, p_gu, x_recv, y_recv, ax_send, ax_recv,
    dx_send, dx_core, dx_z, dx_xl, dx_xlr, dt_send, dt_core, dt_z, dt_xl, dt_xlr,
    load_sem, xs_sem, xr_sem, ys_sem, yr_sem, as_sem, cs_sem, cr_sem, zs_sem, zr_sem,
):
    blk = lax.axis_index("blk")
    dp = lax.axis_index("dp")
    z = blk // 4
    xl = lax.rem(blk // 2, 2)
    core = lax.rem(blk, 2)
    y = dp // 2
    half = lax.rem(dp, 2)
    other = 1 - half

    def at(zz=None, xx=None, cc=None):
        zz = z if zz is None else zz
        xx = xl if xx is None else xx
        cc = core if cc is None else cc
        return (zz * 4 + xx * 2 + cc, dp)

    y_dev = {
        DOWN: (blk, lax.rem(y + NY - 1, NY) * 2 + half),
        UP: (blk, lax.rem(y + 1, NY) * 2 + half),
    }
    x_dev = (blk, y * 2 + other)
    core_dev = at(cc=1 - core)
    xl_dev = at(xx=1 - xl)

    def z_dev(step):
        return at(zz=lax.rem(z + step, NZ))

    loads = [
        pltpu.make_async_copy(src, dst, load_sem.at[i])
        for i, (src, dst) in enumerate(
            ((tok_hbm, tok), (wg_hbm, wg), (wu_hbm, wu), (cot_hbm, cot), (wd_hbm, wd))
        )
    ]
    for load in loads:
        load.start()

    barrier = pltpu.get_barrier_semaphore()
    for partner in (y_dev[DOWN], y_dev[UP], x_dev, core_dev, xl_dev):
        pl.semaphore_signal(barrier, inc=1, device_id=partner, device_id_type=MESH)
    for step in range(1, NZ):
        pl.semaphore_signal(barrier, inc=1, device_id=z_dev(step), device_id_type=MESH)

    blocks = [list_ref[0, k] for k in range(2)]
    live = [(count_ref[0] > k).astype(F32) for k in range(2)]
    is_block = [[(block == j).astype(F32) for j in range(3)] for block in blocks]

    gates_row = jnp.where(slots_ref[...] == 0, probs_ref[0:1, :], probs_ref[1:2, :])
    diagonal = lax.broadcasted_iota(jnp.int32, (BLOCK, BLOCK), 0) == lax.broadcasted_iota(
        jnp.int32, (BLOCK, BLOCK), 1
    )
    columns = [
        jnp.sum(jnp.where(diagonal, gates_row[:, j * BLOCK : (j + 1) * BLOCK], 0.0), axis=1, keepdims=True)
        for j in range(3)
    ]
    for k in range(2):
        column = sum(columns[j] * is_block[k][j] for j in range(3))
        fac[k * BLOCK : (k + 1) * BLOCK, :] = jnp.broadcast_to(column * live[k], (BLOCK, BLOCK))
        for j in range(3):
            picks[k, j] = jnp.broadcast_to(is_block[k][j], (16, 128)).astype(BF)

    def take_rows(source, target):
        def step(i, carry):
            for col in range(0, D, 128):
                parts = [source[pl.ds(pl.multiple_of(j * BLOCK + i * 16, 16), 16), col : col + 128] for j in range(3)]
                for k in range(2):
                    target[pl.ds(pl.multiple_of(k * BLOCK + i * 16, 16), 16), col : col + 128] = (
                        parts[0] * picks[k, 0] + parts[1] * picks[k, 1] + parts[2] * picks[k, 2]
                    )
            return carry

        lax.fori_loop(0, BLOCK // 16, step, 0)

    loads[0].wait()
    take_rows(tok, rin)
    loads[1].wait()
    f_gate[...] = jnp.dot(rin[...], wg[...], preferred_element_type=F32)
    loads[2].wait()
    f_up[...] = jnp.dot(rin[...], wu[...], preferred_element_type=F32)
    loads[3].wait()
    take_rows(cot, rct)

    def factor_rows(rows):
        column = fac[rows, :]
        return jnp.concatenate([column, column, column], axis=1)

    def first_part(i, carry):
        rows = pl.ds(pl.multiple_of(i * 32, 32), 32)
        pre_gate = f_gate[rows, :]
        pre_up = f_up[rows, :]
        sig = jax.nn.sigmoid(pre_gate)
        act = pre_gate * sig
        hidden = (act * pre_up).astype(BF)
        hid[rows, :] = hidden
        scaled[rows, :] = (hidden.astype(F32) * factor_rows(rows)).astype(BF)
        f_gate[rows, :] = pre_up * sig * (1.0 + pre_gate * (1.0 - sig))
        f_up[rows, :] = act
        return carry

    lax.fori_loop(0, ROWS // 32, first_part, 0)

    def dest(i):
        sign = 2 * (i % 2) - 1
        return lax.rem(y + 2 * NY + sign * (4 - (i + 1) // 2), NY)

    def order_of(direction, hop):
        if hop == 4:
            return 0
        return 7 - 2 * hop if direction == UP else 8 - 2 * hop

    def cols_of(t):
        return pl.ds(pl.multiple_of(t * CHUNK, CHUNK), CHUNK)

    def down_partial(i, carry):
        t = dest(i)
        part = dot_lead(rct[:, cols_of(t)], scaled[...]).astype(BF)
        p_down[t, 0] = part[:SHARD]
        p_down[t, 1] = part[SHARD:]
        return carry

    def y_copy(stream, direction, turn, src):
        return pltpu.make_async_remote_copy(
            src_ref=src,
            dst_ref=y_recv.at[stream, direction, turn],
            send_sem=ys_sem.at[stream, direction, turn],
            recv_sem=yr_sem.at[stream, direction, turn],
            device_id=y_dev[direction],
            device_id_type=MESH,
        )

    y_copies = {}

    def y_send(stream, direction, turn, src):
        copy = y_copy(stream, direction, turn, src)
        copy.start()
        y_copies[stream, direction, turn] = copy

    def own(stream, direction, hop):
        i = order_of(direction, hop)
        t = dest(i)
        if stream < 2:
            return p_down[t, other if stream == 0 else half].astype(F32)
        return p_gu[t, half, stream - 2].astype(F32) + x_recv[i, stream - 2].astype(F32)

    def first_turn_down(stream, direction):
        t = dest(order_of(direction, HOPS[stream, direction]))
        y_send(stream, direction, 0, p_down.at[t, other if stream == 0 else half])

    def forward_turn(stream, direction, turn):
        y_copies[stream, direction, turn - 1].wait_recv()
        slot = y_recv.at[stream, direction, turn - 1]
        slot[...] = (slot[...].astype(F32) + own(stream, direction, HOPS[stream, direction] - turn)).astype(BF)
        y_send(stream, direction, turn, slot)

    def last_sum(stream):
        total = own(stream, UP, 0)
        for direction in (DOWN, UP):
            turn = HOPS[stream, direction] - 1
            y_copies[stream, direction, turn].wait_recv()
            total = total + y_recv[stream, direction, turn].astype(F32)
        return total

    lax.fori_loop(0, 3, down_partial, 0)
    pl.semaphore_wait(barrier, 5 + NZ - 1)
    first_turn_down(0, DOWN)
    first_turn_down(1, UP)
    first_turn_down(0, UP)
    first_turn_down(1, DOWN)
    lax.fori_loop(3, NY, down_partial, 0)

    loads[4].wait()
    f_back[...] = jnp.dot(rct[...], wd[...], preferred_element_type=F32)

    def second_part(i, carry):
        rows = pl.ds(pl.multiple_of(i * 32, 32), 32)
        back = f_back[rows, :]
        d_hidden = back * factor_rows(rows)
        dpre[rows, 0:HID] = (d_hidden * f_gate[rows, :]).astype(BF)
        dpre[rows, HID : 2 * HID] = (d_hidden * f_up[rows, :]).astype(BF)
        f_back[rows, :] = hid[rows, :].astype(F32) * back
        return carry

    lax.fori_loop(0, ROWS // 32, second_part, 0)

    def x_copy(i):
        return pltpu.make_async_remote_copy(
            src_ref=p_gu.at[dest(i), other],
            dst_ref=x_recv.at[i],
            send_sem=xs_sem.at[i],
            recv_sem=xr_sem.at[i],
            device_id=x_dev,
            device_id_type=MESH,
        )

    def gu_partial(i, carry):
        t = dest(i)
        part = dot_lead(rin[:, cols_of(t)], dpre[...]).astype(BF)
        for h in range(2):
            for which in range(2):
                p_gu[t, h, which] = part[h * SHARD : (h + 1) * SHARD, which * HID : (which + 1) * HID]
        x_copy(i).start()
        return carry

    lax.fori_loop(0, NY, gu_partial, 0)

    for stream, direction in ((0, DOWN), (1, UP), (0, UP), (1, DOWN)):
        forward_turn(stream, direction, 1)

    def dx_part(q, carry):
        rows = pl.ds(pl.multiple_of(q * CHUNK, CHUNK), CHUNK)
        part = (dot_last(wg[rows, :], dpre[:, 0:HID]) + dot_last(wu[rows, :], dpre[:, HID : 2 * HID])).astype(BF)
        for m in range(6):
            dx_send[m % 2, 3 * q + m // 2] = part[m * FEAT : (m + 1) * FEAT]
        return carry

    lax.fori_loop(0, D // CHUNK, dx_part, 0)
    folded = f_back[:, 0:128] + f_back[:, 128:256] + f_back[:, 256:384]
    dots = jnp.sum(folded.T, axis=0, keepdims=True)
    dt_send[...] = jnp.broadcast_to(dots, (8, ROWS))

    def plain_copy(src, dst, send, recv, device):
        copy = pltpu.make_async_remote_copy(
            src_ref=src, dst_ref=dst, send_sem=send, recv_sem=recv, device_id=device, device_id_type=MESH
        )
        copy.start()
        return copy

    dx_core_copy = plain_copy(dx_send.at[1 - core], dx_core, cs_sem.at[0], cr_sem.at[0], core_dev)
    dt_core_copy = plain_copy(dt_send, dt_core, cs_sem.at[1], cr_sem.at[1], core_dev)

    def first_turn_gu(stream, direction):
        i = order_of(direction, HOPS[stream, direction])
        slot = x_recv.at[i, stream - 2]
        slot[...] = own(stream, direction, HOPS[stream, direction]).astype(BF)
        y_send(stream, direction, 0, slot)

    def x_arrived(i):
        x_copy(i).wait_recv()

    x_arrived(0)
    first_turn_gu(2, DOWN)
    first_turn_gu(3, UP)
    x_arrived(1)
    x_arrived(2)
    first_turn_gu(2, UP)
    first_turn_gu(3, DOWN)

    dx_core_copy.wait_recv()
    dt_core_copy.wait_recv()

    def add_core(i, carry):
        dx_core[i] = (dx_core[i].astype(F32) + dx_send[core, i].astype(F32)).astype(BF)
        return carry

    lax.fori_loop(0, 2 * NZ, add_core, 0)
    dt_z[0] = dt_send[...] + dt_core[...]

    def z_copy(step):
        target = lax.rem(z + step, NZ)
        return pltpu.make_async_remote_copy(
            src_ref=dx_core.at[pl.ds(2 * target, 2)],
            dst_ref=dx_z.at[step],
            send_sem=zs_sem.at[0, step],
            recv_sem=zr_sem.at[0, step],
            device_id=z_dev(step),
            device_id_type=MESH,
        )

    def z_dot_copy(step):
        return pltpu.make_async_remote_copy(
            src_ref=dt_z.at[0],
            dst_ref=dt_z.at[step],
            send_sem=zs_sem.at[1, step],
            recv_sem=zr_sem.at[1, step],
            device_id=z_dev(step),
            device_id_type=MESH,
        )

    def z_start(step, carry):
        z_copy(step).start()
        z_dot_copy(step).start()
        return carry

    lax.fori_loop(1, NZ, z_start, 0)

    for stream, direction in ((0, DOWN), (1, UP), (0, UP), (1, DOWN)):
        forward_turn(stream, direction, 2)
    x_arrived(3)
    x_arrived(4)
    for stream, direction in ((2, DOWN), (3, UP), (2, UP), (3, DOWN)):
        forward_turn(stream, direction, 1)
    forward_turn(0, DOWN, 3)
    forward_turn(1, UP, 3)

    def z_wait(step, carry):
        z_copy(step).wait_recv()
        z_dot_copy(step).wait_recv()
        return carry

    lax.fori_loop(1, NZ, z_wait, 0)

    def z_sum(step, total):
        return total + dx_z[step].astype(F32)

    dx_sum = lax.fori_loop(1, NZ, z_sum, dx_core[pl.ds(2 * z, 2)].astype(F32))
    dots = dt_z[z]
    for source in range(1, NZ):
        dots = dots + dt_z[lax.rem(z + NZ - source, NZ)]
    f_back[0:FEAT, 0:ROWS] = dx_sum[0]
    f_back[FEAT : 2 * FEAT, 0:ROWS] = dx_sum[1]
    dx_xl[...] = f_back[pl.ds(pl.multiple_of((1 - xl) * FEAT, FEAT), FEAT), 0:ROWS].astype(BF)
    dt_xl[...] = dots
    dx_xl_copy = plain_copy(dx_xl, dx_xlr, cs_sem.at[2], cr_sem.at[2], xl_dev)
    dt_xl_copy = plain_copy(dt_xl, dt_xlr, cs_sem.at[3], cr_sem.at[3], xl_dev)

    ax_send[...] = last_sum(0).astype(BF)
    ax_copy = plain_copy(ax_send, ax_recv, as_sem.at[0], as_sem.at[1], x_dev)

    x_arrived(5)
    x_arrived(6)
    for stream, direction in ((2, DOWN), (3, UP), (2, UP), (3, DOWN)):
        forward_turn(stream, direction, 2)

    dx_xl_copy.wait_recv()
    dt_xl_copy.wait_recv()
    grads = f_back[pl.ds(pl.multiple_of(xl * FEAT, FEAT), FEAT), 0:ROWS] + dx_xlr[...].astype(F32)
    dots = dt_xl[0:1, :] + dt_xlr[0:1, :]
    for j in range(3):
        block_cols = slice(j * BLOCK, (j + 1) * BLOCK)
        gtok_out[:, block_cols] = (
            grads[:, 0:BLOCK] * is_block[0][j] + grads[:, BLOCK:ROWS] * is_block[1][j]
        ).astype(BF)
        values = dots[:, 0:BLOCK] * (is_block[0][j] * live[0]) + dots[:, BLOCK:ROWS] * (is_block[1][j] * live[1])
        slots = slots_ref[:, block_cols]
        gprob_out[0:1, block_cols] = jnp.where(slots == 0, values, 0.0)
        gprob_out[1:2, block_cols] = jnp.where(slots == 1, values, 0.0)

    forward_turn(2, DOWN, 3)
    forward_turn(3, UP, 3)
    down_sum = last_sum(1)
    ax_copy.wait_recv()
    gd_out[...] = (down_sum + ax_recv[...].astype(F32)).astype(BF)
    x_arrived(7)
    gg_out[...] = last_sum(2).astype(BF)
    gu_out[...] = last_sum(3).astype(BF)

    for copy in y_copies.values():
        copy.wait_send()
    for copy in (dx_core_copy, dt_core_copy, dx_xl_copy, dt_xl_copy, ax_copy):
        copy.wait_send()

    def sent(i, carry):
        x_copy(i).wait_send()
        return carry

    lax.fori_loop(0, NY, sent, 0)

    def z_sent(step, carry):
        z_copy(step).wait_send()
        z_dot_copy(step).wait_send()
        return carry

    lax.fori_loop(1, NZ, z_sent, 0)


def body(tokens, cotangent, w_gate, w_up, w_down_t, gate_probs, slot_ids, block_list, block_count):
    smem = pl.BlockSpec(memory_space=pltpu.SMEM)
    vmem = pl.BlockSpec(memory_space=pltpu.VMEM)
    anywhere = pl.BlockSpec(memory_space=pl.ANY)
    dma = pltpu.SemaphoreType.DMA
    shard = (SHARD, HID)
    gtok, gprob, gg, gu, gd = pl.pallas_call(
        kernel,
        out_shape=(
            jax.ShapeDtypeStruct((FEAT, TOK), BF),
            jax.ShapeDtypeStruct((2, TOK), F32),
            jax.ShapeDtypeStruct(shard, BF),
            jax.ShapeDtypeStruct(shard, BF),
            jax.ShapeDtypeStruct(shard, BF),
        ),
        in_specs=[smem, smem, vmem, vmem] + [anywhere] * 5,
        out_specs=(vmem,) * 5,
        scratch_shapes=[
            pltpu.VMEM((TOK, D), BF),
            pltpu.VMEM((TOK, D), BF),
            pltpu.VMEM((D, HID), BF),
            pltpu.VMEM((D, HID), BF),
            pltpu.VMEM((D, HID), BF),
            pltpu.VMEM((ROWS, D), BF),
            pltpu.VMEM((ROWS, D), BF),
            pltpu.VMEM((ROWS, HID), F32),
            pltpu.VMEM((ROWS, HID), F32),
            pltpu.VMEM((ROWS, HID), F32),
            pltpu.VMEM((ROWS, HID), BF),
            pltpu.VMEM((ROWS, HID), BF),
            pltpu.VMEM((ROWS, 2 * HID), BF),
            pltpu.VMEM((ROWS, BLOCK), F32),
            pltpu.VMEM((2, 3, 16, 128), BF),
            pltpu.VMEM((NY, 2) + shard, BF),
            pltpu.VMEM((NY, 2, 2) + shard, BF),
            pltpu.VMEM((NY, 2) + shard, BF),
            pltpu.VMEM((4, 2, 4) + shard, BF),
            pltpu.VMEM(shard, BF),
            pltpu.VMEM(shard, BF),
            pltpu.VMEM((2, 2 * NZ, FEAT, ROWS), BF),
            pltpu.VMEM((2 * NZ, FEAT, ROWS), BF),
            pltpu.VMEM((NZ, 2, FEAT, ROWS), BF),
            pltpu.VMEM((FEAT, ROWS), BF),
            pltpu.VMEM((FEAT, ROWS), BF),
            pltpu.VMEM((8, ROWS), F32),
            pltpu.VMEM((8, ROWS), F32),
            pltpu.VMEM((NZ, 8, ROWS), F32),
            pltpu.VMEM((8, ROWS), F32),
            pltpu.VMEM((8, ROWS), F32),
            dma((5,)),
            dma((NY,)),
            dma((NY,)),
            dma((4, 2, 4)),
            dma((4, 2, 4)),
            dma((2,)),
            dma((4,)),
            dma((4,)),
            dma((2, NZ)),
            dma((2, NZ)),
        ],
        compiler_params=pltpu.CompilerParams(
            collective_id=0, has_side_effects=True, vmem_limit_bytes=52 * 1024 * 1024
        ),
        name="expert_backward",
    )(
        block_list, block_count, gate_probs.T, slot_ids.reshape(1, TOK),
        tokens, cotangent, w_gate, w_up, w_down_t,
    )
    return gtok.T, gprob.T, gg, gu, gd


def solution(mesh):
    placed = (
        P("dp", None),
        P("dp", None),
        P(None, "blk"),
        P(None, "blk"),
        P(None, "blk"),
        P("dp", None),
        P("dp"),
        P("dp", None),
        P("dp"),
    )
    return jax.shard_map(
        body,
        mesh=mesh,
        in_specs=placed,
        out_specs=(P("dp", "blk"), P("dp", None), P("dp", "blk"), P("dp", "blk"), P("dp", "blk")),
        check_vma=False,
    )
```

```python
import jax
import jax.numpy as jnp
from jax import lax
from jax.experimental import pallas as pl
from jax.experimental.pallas import tpu as pltpu
from jax.sharding import PartitionSpec as P

MESH = pl.DeviceIdType.MESH
BF = jnp.bfloat16
F32 = jnp.float32

D = 3072
HID = 384
BLOCK = 128
TOK = 384
ROWS = 256
NY = 8
NZ = 12
SHARD = 192
FEAT = 64
CHUNK = 384

DOWN, UP = 0, 1
HOPS = {(0, DOWN): 4, (0, UP): 3, (1, DOWN): 3, (1, UP): 4, (2, DOWN): 4, (2, UP): 3, (3, DOWN): 3, (3, UP): 4}


def dot_lead(left, right):
    return lax.dot_general(left, right, (((0,), (0,)), ((), ())), preferred_element_type=F32)


def dot_last(left, right):
    return lax.dot_general(left, right, (((1,), (1,)), ((), ())), preferred_element_type=F32)


def kernel(
    list_ref, count_ref, probs_ref, slots_ref, tok_hbm, cot_hbm, wg_hbm, wu_hbm, wd_hbm,
    gtok_out, gprob_out, gg_out, gu_out, gd_out,
    tok, cot, wgu, wd, rin, rct, f_gu, f_back, hid, scaled, dpre, fac, picks,
    rows_t, rows_x, dpre_x, p_down, p_gu, y_recv, ax_send, ax_recv,
    dx_send, dx_core, dx_z, dx_xl, dx_xlr, dt_send, dt_core, dt_z, dt_xl, dt_xlr,
    load_sem, xs_sem, xr_sem, ys_sem, yr_sem, as_sem, cs_sem, cr_sem, zs_sem, zr_sem,
):
    blk = lax.axis_index("blk")
    dp = lax.axis_index("dp")
    z = blk // 4
    xl = lax.rem(blk // 2, 2)
    core = lax.rem(blk, 2)
    y = dp // 2
    half = lax.rem(dp, 2)
    other = 1 - half

    def at(zz=None, xx=None, cc=None):
        zz = z if zz is None else zz
        xx = xl if xx is None else xx
        cc = core if cc is None else cc
        return (zz * 4 + xx * 2 + cc, dp)

    y_dev = {
        DOWN: (blk, lax.rem(y + NY - 1, NY) * 2 + half),
        UP: (blk, lax.rem(y + 1, NY) * 2 + half),
    }
    x_dev = (blk, y * 2 + other)
    core_dev = at(cc=1 - core)
    xl_dev = at(xx=1 - xl)

    def z_dev(step):
        return at(zz=lax.rem(z + step, NZ))

    loads = [
        pltpu.make_async_copy(src, dst, load_sem.at[i])
        for i, (src, dst) in enumerate(
            (
                (tok_hbm, tok),
                (wg_hbm, wgu.at[:, 0:HID]),
                (wu_hbm, wgu.at[:, HID : 2 * HID]),
                (cot_hbm, cot),
                (wd_hbm, wd),
            )
        )
    ]
    for load in loads:
        load.start()

    barrier = pltpu.get_barrier_semaphore()
    for partner in (y_dev[DOWN], y_dev[UP], x_dev, core_dev, xl_dev):
        pl.semaphore_signal(barrier, inc=1, device_id=partner, device_id_type=MESH)
    for step in range(1, NZ):
        pl.semaphore_signal(barrier, inc=1, device_id=z_dev(step), device_id_type=MESH)

    blocks = [list_ref[0, k] for k in range(2)]
    live = [(count_ref[0] > k).astype(F32) for k in range(2)]
    is_block = [[(block == j).astype(F32) for j in range(3)] for block in blocks]

    gates_row = jnp.where(slots_ref[...] == 0, probs_ref[0:1, :], probs_ref[1:2, :])
    diagonal = lax.broadcasted_iota(jnp.int32, (BLOCK, BLOCK), 0) == lax.broadcasted_iota(
        jnp.int32, (BLOCK, BLOCK), 1
    )
    columns = [
        jnp.sum(jnp.where(diagonal, gates_row[:, j * BLOCK : (j + 1) * BLOCK], 0.0), axis=1, keepdims=True)
        for j in range(3)
    ]
    for k in range(2):
        column = sum(columns[j] * is_block[k][j] for j in range(3))
        fac[k * BLOCK : (k + 1) * BLOCK, :] = jnp.broadcast_to(column * live[k], (BLOCK, BLOCK))
        for j in range(3):
            picks[k, j] = jnp.broadcast_to(is_block[k][j], (16, 128)).astype(BF)

    def take_rows(source, target):
        def step(i, carry):
            for col in range(0, D, 128):
                parts = [source[pl.ds(pl.multiple_of(j * BLOCK + i * 16, 16), 16), col : col + 128] for j in range(3)]
                for k in range(2):
                    target[pl.ds(pl.multiple_of(k * BLOCK + i * 16, 16), 16), col : col + 128] = (
                        parts[0] * picks[k, 0] + parts[1] * picks[k, 1] + parts[2] * picks[k, 2]
                    )
            return carry

        lax.fori_loop(0, BLOCK // 16, step, 0)

    loads[0].wait()
    take_rows(tok, rin)

    def cols_of(t):
        return pl.ds(pl.multiple_of(t * CHUNK, CHUNK), CHUNK)

    def turn_rows(t, carry):
        part = rin[:, cols_of(t)].T
        rows_t[t, 0] = part[:SHARD]
        rows_t[t, 1] = part[SHARD:]
        return carry

    lax.fori_loop(0, NY, turn_rows, 0)
    pl.semaphore_wait(barrier, 5 + NZ - 1)

    def plain_copy(src, dst, send, recv, device):
        copy = pltpu.make_async_remote_copy(
            src_ref=src, dst_ref=dst, send_sem=send, recv_sem=recv, device_id=device, device_id_type=MESH
        )
        copy.start()
        return copy

    rows_copy = plain_copy(rows_t.at[:, other], rows_x, xs_sem.at[0], xr_sem.at[0], x_dev)

    loads[1].wait()
    loads[2].wait()
    f_gu[...] = jnp.dot(rin[...], wgu[...], preferred_element_type=F32)
    loads[3].wait()
    take_rows(cot, rct)

    def factor_rows(rows):
        column = fac[rows, :]
        return jnp.concatenate([column, column, column], axis=1)

    def first_part(i, carry):
        rows = pl.ds(pl.multiple_of(i * 32, 32), 32)
        pre_gate = f_gu[rows, 0:HID]
        pre_up = f_gu[rows, HID : 2 * HID]
        sig = jax.nn.sigmoid(pre_gate)
        act = pre_gate * sig
        hidden = (act * pre_up).astype(BF)
        hid[rows, :] = hidden
        scaled[rows, :] = (hidden.astype(F32) * factor_rows(rows)).astype(BF)
        f_gu[rows, 0:HID] = pre_up * sig * (1.0 + pre_gate * (1.0 - sig))
        f_gu[rows, HID : 2 * HID] = act
        return carry

    lax.fori_loop(0, ROWS // 32, first_part, 0)

    def dest(i):
        sign = 2 * (i % 2) - 1
        return lax.rem(y + 2 * NY + sign * (4 - (i + 1) // 2), NY)

    def order_of(direction, hop):
        if hop == 4:
            return 0
        return 7 - 2 * hop if direction == UP else 8 - 2 * hop

    def down_partial(i, carry):
        t = dest(i)
        part = dot_lead(rct[:, cols_of(t)], scaled[...]).astype(BF)
        p_down[t, 0] = part[:SHARD]
        p_down[t, 1] = part[SHARD:]
        return carry

    def y_copy(stream, direction, turn, src):
        return pltpu.make_async_remote_copy(
            src_ref=src,
            dst_ref=y_recv.at[stream, direction, turn],
            send_sem=ys_sem.at[stream, direction, turn],
            recv_sem=yr_sem.at[stream, direction, turn],
            device_id=y_dev[direction],
            device_id_type=MESH,
        )

    y_copies = {}

    def y_send(stream, direction, turn, src):
        copy = y_copy(stream, direction, turn, src)
        copy.start()
        y_copies[stream, direction, turn] = copy

    def own(stream, direction, hop):
        i = order_of(direction, hop)
        t = dest(i)
        if stream < 2:
            return p_down[t, other if stream == 0 else half].astype(F32)
        return p_gu[t, stream - 2].astype(F32)

    def first_turn(stream, direction):
        t = dest(order_of(direction, HOPS[stream, direction]))
        if stream < 2:
            y_send(stream, direction, 0, p_down.at[t, other if stream == 0 else half])
        else:
            y_send(stream, direction, 0, p_gu.at[t, stream - 2])

    def forward_turn(stream, direction, turn):
        y_copies[stream, direction, turn - 1].wait_recv()
        slot = y_recv.at[stream, direction, turn - 1]
        slot[...] = (slot[...].astype(F32) + own(stream, direction, HOPS[stream, direction] - turn)).astype(BF)
        y_send(stream, direction, turn, slot)

    def last_sum(stream):
        total = own(stream, UP, 0)
        for direction in (DOWN, UP):
            turn = HOPS[stream, direction] - 1
            y_copies[stream, direction, turn].wait_recv()
            total = total + y_recv[stream, direction, turn].astype(F32)
        return total

    lax.fori_loop(0, 3, down_partial, 0)
    for stream, direction in ((0, DOWN), (1, UP), (0, UP), (1, DOWN)):
        first_turn(stream, direction)
    lax.fori_loop(3, NY, down_partial, 0)

    loads[4].wait()
    f_back[...] = jnp.dot(rct[...], wd[...], preferred_element_type=F32)

    def second_part(i, carry):
        rows = pl.ds(pl.multiple_of(i * 32, 32), 32)
        back = f_back[rows, :]
        d_hidden = back * factor_rows(rows)
        dpre[rows, 0:HID] = (d_hidden * f_gu[rows, 0:HID]).astype(BF)
        dpre[rows, HID : 2 * HID] = (d_hidden * f_gu[rows, HID : 2 * HID]).astype(BF)
        f_back[rows, :] = hid[rows, :].astype(F32) * back
        return carry

    lax.fori_loop(0, ROWS // 32, second_part, 0)

    dpre_copy = plain_copy(dpre, dpre_x, xs_sem.at[1], xr_sem.at[1], x_dev)

    def gu_partial(i, carry):
        t = dest(i)
        part = (
            jnp.dot(rows_t[t, half], dpre[...], preferred_element_type=F32)
            + jnp.dot(rows_x[t], dpre_x[...], preferred_element_type=F32)
        ).astype(BF)
        p_gu[t, 0] = part[:, 0:HID]
        p_gu[t, 1] = part[:, HID : 2 * HID]
        return carry

    for stream, direction in ((0, DOWN), (1, UP), (0, UP), (1, DOWN)):
        forward_turn(stream, direction, 1)

    def dx_part(q, carry):
        rows = pl.ds(pl.multiple_of(q * CHUNK, CHUNK), CHUNK)
        part = dot_last(wgu[rows, :], dpre[...]).astype(BF)
        for m in range(6):
            dx_send[m % 2, 3 * q + m // 2] = part[m * FEAT : (m + 1) * FEAT]
        return carry

    lax.fori_loop(0, D // CHUNK, dx_part, 0)
    folded = f_back[:, 0:128] + f_back[:, 128:256] + f_back[:, 256:384]
    dots = jnp.sum(folded.T, axis=0, keepdims=True)
    dt_send[...] = jnp.broadcast_to(dots, (8, ROWS))

    dx_core_copy = plain_copy(dx_send.at[1 - core], dx_core, cs_sem.at[0], cr_sem.at[0], core_dev)
    dt_core_copy = plain_copy(dt_send, dt_core, cs_sem.at[1], cr_sem.at[1], core_dev)

    for stream, direction in ((0, DOWN), (1, UP), (0, UP), (1, DOWN)):
        forward_turn(stream, direction, 2)

    rows_copy.wait_recv()
    dpre_copy.wait_recv()
    lax.fori_loop(0, 3, gu_partial, 0)
    for stream, direction in ((2, DOWN), (3, UP), (2, UP), (3, DOWN)):
        first_turn(stream, direction)
    lax.fori_loop(3, NY, gu_partial, 0)

    dx_core_copy.wait_recv()
    dt_core_copy.wait_recv()

    def add_core(i, carry):
        dx_core[i] = (dx_core[i].astype(F32) + dx_send[core, i].astype(F32)).astype(BF)
        return carry

    lax.fori_loop(0, 2 * NZ, add_core, 0)
    dt_z[0] = dt_send[...] + dt_core[...]

    def z_copy(step):
        target = lax.rem(z + step, NZ)
        return pltpu.make_async_remote_copy(
            src_ref=dx_core.at[pl.ds(2 * target, 2)],
            dst_ref=dx_z.at[step],
            send_sem=zs_sem.at[0, step],
            recv_sem=zr_sem.at[0, step],
            device_id=z_dev(step),
            device_id_type=MESH,
        )

    def z_dot_copy(step):
        return pltpu.make_async_remote_copy(
            src_ref=dt_z.at[0],
            dst_ref=dt_z.at[step],
            send_sem=zs_sem.at[1, step],
            recv_sem=zr_sem.at[1, step],
            device_id=z_dev(step),
            device_id_type=MESH,
        )

    def z_start(step, carry):
        z_copy(step).start()
        z_dot_copy(step).start()
        return carry

    lax.fori_loop(1, NZ, z_start, 0)

    forward_turn(0, DOWN, 3)
    forward_turn(1, UP, 3)
    for stream, direction in ((2, DOWN), (3, UP), (2, UP), (3, DOWN)):
        forward_turn(stream, direction, 1)

    def z_wait(step, carry):
        z_copy(step).wait_recv()
        z_dot_copy(step).wait_recv()
        return carry

    lax.fori_loop(1, NZ, z_wait, 0)

    def z_sum(step, total):
        return total + dx_z[step].astype(F32)

    dx_sum = lax.fori_loop(1, NZ, z_sum, dx_core[pl.ds(2 * z, 2)].astype(F32))
    dots = dt_z[z]
    for source in range(1, NZ):
        dots = dots + dt_z[lax.rem(z + NZ - source, NZ)]
    f_back[0:FEAT, 0:ROWS] = dx_sum[0]
    f_back[FEAT : 2 * FEAT, 0:ROWS] = dx_sum[1]
    dx_xl[...] = f_back[pl.ds(pl.multiple_of((1 - xl) * FEAT, FEAT), FEAT), 0:ROWS].astype(BF)
    dt_xl[...] = dots
    dx_xl_copy = plain_copy(dx_xl, dx_xlr, cs_sem.at[2], cr_sem.at[2], xl_dev)
    dt_xl_copy = plain_copy(dt_xl, dt_xlr, cs_sem.at[3], cr_sem.at[3], xl_dev)

    ax_send[...] = last_sum(0).astype(BF)
    ax_copy = plain_copy(ax_send, ax_recv, as_sem.at[0], as_sem.at[1], x_dev)

    for stream, direction in ((2, DOWN), (3, UP), (2, UP), (3, DOWN)):
        forward_turn(stream, direction, 2)

    dx_xl_copy.wait_recv()
    dt_xl_copy.wait_recv()
    grads = f_back[pl.ds(pl.multiple_of(xl * FEAT, FEAT), FEAT), 0:ROWS] + dx_xlr[...].astype(F32)
    dots = dt_xl[0:1, :] + dt_xlr[0:1, :]
    for j in range(3):
        block_cols = slice(j * BLOCK, (j + 1) * BLOCK)
        gtok_out[:, block_cols] = (
            grads[:, 0:BLOCK] * is_block[0][j] + grads[:, BLOCK:ROWS] * is_block[1][j]
        ).astype(BF)
        values = dots[:, 0:BLOCK] * (is_block[0][j] * live[0]) + dots[:, BLOCK:ROWS] * (is_block[1][j] * live[1])
        slots = slots_ref[:, block_cols]
        gprob_out[0:1, block_cols] = jnp.where(slots == 0, values, 0.0)
        gprob_out[1:2, block_cols] = jnp.where(slots == 1, values, 0.0)

    forward_turn(2, DOWN, 3)
    forward_turn(3, UP, 3)
    down_sum = last_sum(1)
    ax_copy.wait_recv()
    gd_out[...] = (down_sum + ax_recv[...].astype(F32)).astype(BF)
    gg_out[...] = last_sum(2).astype(BF)
    gu_out[...] = last_sum(3).astype(BF)

    for copy in y_copies.values():
        copy.wait_send()
    for copy in (rows_copy, dpre_copy, dx_core_copy, dt_core_copy, dx_xl_copy, dt_xl_copy, ax_copy):
        copy.wait_send()

    def z_sent(step, carry):
        z_copy(step).wait_send()
        z_dot_copy(step).wait_send()
        return carry

    lax.fori_loop(1, NZ, z_sent, 0)


def body(tokens, cotangent, w_gate, w_up, w_down_t, gate_probs, slot_ids, block_list, block_count):
    smem = pl.BlockSpec(memory_space=pltpu.SMEM)
    vmem = pl.BlockSpec(memory_space=pltpu.VMEM)
    anywhere = pl.BlockSpec(memory_space=pl.ANY)
    dma = pltpu.SemaphoreType.DMA
    shard = (SHARD, HID)
    gtok, gprob, gg, gu, gd = pl.pallas_call(
        kernel,
        out_shape=(
            jax.ShapeDtypeStruct((FEAT, TOK), BF),
            jax.ShapeDtypeStruct((2, TOK), F32),
            jax.ShapeDtypeStruct(shard, BF),
            jax.ShapeDtypeStruct(shard, BF),
            jax.ShapeDtypeStruct(shard, BF),
        ),
        in_specs=[smem, smem, vmem, vmem] + [anywhere] * 5,
        out_specs=(vmem,) * 5,
        scratch_shapes=[
            pltpu.VMEM((TOK, D), BF),
            pltpu.VMEM((TOK, D), BF),
            pltpu.VMEM((D, 2 * HID), BF),
            pltpu.VMEM((D, HID), BF),
            pltpu.VMEM((ROWS, D), BF),
            pltpu.VMEM((ROWS, D), BF),
            pltpu.VMEM((ROWS, 2 * HID), F32),
            pltpu.VMEM((ROWS, HID), F32),
            pltpu.VMEM((ROWS, HID), BF),
            pltpu.VMEM((ROWS, HID), BF),
            pltpu.VMEM((ROWS, 2 * HID), BF),
            pltpu.VMEM((ROWS, BLOCK), F32),
            pltpu.VMEM((2, 3, 16, 128), BF),
            pltpu.VMEM((NY, 2, SHARD, ROWS), BF),
            pltpu.VMEM((NY, SHARD, ROWS), BF),
            pltpu.VMEM((ROWS, 2 * HID), BF),
            pltpu.VMEM((NY, 2) + shard, BF),
            pltpu.VMEM((NY, 2) + shard, BF),
            pltpu.VMEM((4, 2, 4) + shard, BF),
            pltpu.VMEM(shard, BF),
            pltpu.VMEM(shard, BF),
            pltpu.VMEM((2, 2 * NZ, FEAT, ROWS), BF),
            pltpu.VMEM((2 * NZ, FEAT, ROWS), BF),
            pltpu.VMEM((NZ, 2, FEAT, ROWS), BF),
            pltpu.VMEM((FEAT, ROWS), BF),
            pltpu.VMEM((FEAT, ROWS), BF),
            pltpu.VMEM((8, ROWS), F32),
            pltpu.VMEM((8, ROWS), F32),
            pltpu.VMEM((NZ, 8, ROWS), F32),
            pltpu.VMEM((8, ROWS), F32),
            pltpu.VMEM((8, ROWS), F32),
            dma((5,)),
            dma((2,)),
            dma((2,)),
            dma((4, 2, 4)),
            dma((4, 2, 4)),
            dma((2,)),
            dma((4,)),
            dma((4,)),
            dma((2, NZ)),
            dma((2, NZ)),
        ],
        compiler_params=pltpu.CompilerParams(
            collective_id=0, has_side_effects=True, vmem_limit_bytes=52 * 1024 * 1024
        ),
        name="expert_backward",
    )(
        block_list, block_count, gate_probs.T, slot_ids.reshape(1, TOK),
        tokens, cotangent, w_gate, w_up, w_down_t,
    )
    return gtok.T, gprob.T, gg, gu, gd


def solution(mesh):
    placed = (
        P("dp", None),
        P("dp", None),
        P(None, "blk"),
        P(None, "blk"),
        P(None, "blk"),
        P("dp", None),
        P("dp"),
        P("dp", None),
        P("dp"),
    )
    return jax.shard_map(
        body,
        mesh=mesh,
        in_specs=placed,
        out_specs=(P("dp", "blk"), P("dp", None), P("dp", "blk"), P("dp", "blk"), P("dp", "blk")),
        check_vma=False,
    )
```

```python
import jax
import jax.numpy as jnp
from jax import lax
from jax.experimental import pallas as pl
from jax.experimental.pallas import tpu as pltpu
from jax.sharding import PartitionSpec as P

MESH = pl.DeviceIdType.MESH
BF = jnp.bfloat16
F32 = jnp.float32

D = 3072
HID = 384
BLOCK = 128
TOK = 384
ROWS = 256
NY = 8
NZ = 12
SHARD = 192
FEAT = 64
CHUNK = 384

DOWN, UP = 0, 1
HOPS = {(0, DOWN): 4, (0, UP): 3, (1, DOWN): 3, (1, UP): 4, (2, DOWN): 4, (2, UP): 3, (3, DOWN): 3, (3, UP): 4}


def dot_lead(left, right):
    return lax.dot_general(left, right, (((0,), (0,)), ((), ())), preferred_element_type=F32)


def dot_last(left, right):
    return lax.dot_general(left, right, (((1,), (1,)), ((), ())), preferred_element_type=F32)


def kernel(
    list_ref, count_ref, probs_ref, slots_ref, tok_hbm, cot_hbm, wg_hbm, wu_hbm, wd_hbm,
    gtok_out, gprob_out, gg_out, gu_out, gd_out,
    tok, cot, wgu, wd, rin, rct, f_gu, f_back, hid, scaled, dpre, fac, picks,
    rows_t, rows_x, dpre_x, p_down, p_gu, y_recv, ax_send, ax_recv,
    dx_own, dx_core, dx_xl, dx_z, dx_out, dx_fin, dt_own, dt_core, dt_sum, dt_xl, dt_z, dt_out, dt_fin,
    load_sem, xs_sem, xr_sem, ys_sem, yr_sem, as_sem, cs_sem, cr_sem, zs_sem, zr_sem, ready,
):
    blk = lax.axis_index("blk")
    dp = lax.axis_index("dp")
    z = blk // 4
    xl = lax.rem(blk // 2, 2)
    core = lax.rem(blk, 2)
    y = dp // 2
    half = lax.rem(dp, 2)
    other = 1 - half
    colour = lax.rem(y + half + xl + core, 2)

    def at(zz=None, xx=None, cc=None):
        zz = z if zz is None else zz
        xx = xl if xx is None else xx
        cc = core if cc is None else cc
        return (zz * 4 + xx * 2 + cc, dp)

    y_dev = {
        DOWN: (blk, lax.rem(y + NY - 1, NY) * 2 + half),
        UP: (blk, lax.rem(y + 1, NY) * 2 + half),
    }
    x_dev = (blk, y * 2 + other)
    core_dev = at(cc=1 - core)
    xl_dev = at(xx=1 - xl)

    def z_dev(step):
        return at(zz=lax.rem(z + step, NZ))

    loads = [
        pltpu.make_async_copy(src, dst, load_sem.at[i])
        for i, (src, dst) in enumerate(
            (
                (tok_hbm, tok),
                (wg_hbm, wgu.at[:, 0:HID]),
                (wu_hbm, wgu.at[:, HID : 2 * HID]),
                (cot_hbm, cot),
                (wd_hbm, wd),
            )
        )
    ]
    for load in loads:
        load.start()

    plane = (y_dev[DOWN], y_dev[UP], x_dev, core_dev, xl_dev)
    barrier = pltpu.get_barrier_semaphore()

    @pl.when(colour == 0)
    def _():
        for partner in plane:
            pl.semaphore_signal(barrier, inc=1, device_id=partner, device_id_type=MESH)
        for step in range(1, NZ):
            pl.semaphore_signal(barrier, inc=1, device_id=z_dev(step), device_id_type=MESH)

    blocks = [list_ref[0, k] for k in range(2)]
    live = [(count_ref[0] > k).astype(F32) for k in range(2)]
    is_block = [[(block == j).astype(F32) for j in range(3)] for block in blocks]

    gates_row = jnp.where(slots_ref[...] == 0, probs_ref[0:1, :], probs_ref[1:2, :])
    diagonal = lax.broadcasted_iota(jnp.int32, (BLOCK, BLOCK), 0) == lax.broadcasted_iota(
        jnp.int32, (BLOCK, BLOCK), 1
    )
    columns = [
        jnp.sum(jnp.where(diagonal, gates_row[:, j * BLOCK : (j + 1) * BLOCK], 0.0), axis=1, keepdims=True)
        for j in range(3)
    ]
    for k in range(2):
        column = sum(columns[j] * is_block[k][j] for j in range(3))
        fac[k * BLOCK : (k + 1) * BLOCK, :] = jnp.broadcast_to(column * live[k], (BLOCK, BLOCK))
        for j in range(3):
            picks[k, j] = jnp.broadcast_to(is_block[k][j], (16, 128)).astype(BF)

    def take_rows(source, target):
        def step(i, carry):
            for col in range(0, D, 128):
                parts = [source[pl.ds(pl.multiple_of(j * BLOCK + i * 16, 16), 16), col : col + 128] for j in range(3)]
                for k in range(2):
                    target[pl.ds(pl.multiple_of(k * BLOCK + i * 16, 16), 16), col : col + 128] = (
                        parts[0] * picks[k, 0] + parts[1] * picks[k, 1] + parts[2] * picks[k, 2]
                    )
            return carry

        lax.fori_loop(0, BLOCK // 16, step, 0)

    loads[0].wait()
    take_rows(tok, rin)

    @pl.when(colour == 1)
    def _():
        pl.semaphore_wait(barrier, len(plane))
        for partner in plane:
            pl.semaphore_signal(ready, inc=1, device_id=partner, device_id_type=MESH)

    def cols_of(t):
        return pl.ds(pl.multiple_of(t * CHUNK, CHUNK), CHUNK)

    def turn_rows(t, carry):
        part = rin[:, cols_of(t)].T
        rows_t[t, 0] = part[:SHARD]
        rows_t[t, 1] = part[SHARD:]
        return carry

    lax.fori_loop(0, NY, turn_rows, 0)

    @pl.when(colour == 0)
    def _():
        pl.semaphore_wait(ready, len(plane))


    def plain_copy(src, dst, send, recv, device):
        copy = pltpu.make_async_remote_copy(
            src_ref=src, dst_ref=dst, send_sem=send, recv_sem=recv, device_id=device, device_id_type=MESH
        )
        copy.start()
        return copy

    mine = pl.ds((NY // 2) * core, NY // 2)
    rows_copy = plain_copy(rows_t.at[mine, other], rows_x.at[mine], xs_sem.at[0], xr_sem.at[0], x_dev)

    loads[1].wait()
    loads[2].wait()
    f_gu[...] = jnp.dot(rin[...], wgu[...], preferred_element_type=F32)
    loads[3].wait()
    take_rows(cot, rct)

    def factor_rows(rows):
        column = fac[rows, :]
        return jnp.concatenate([column, column, column], axis=1)

    def first_part(i, carry):
        rows = pl.ds(pl.multiple_of(i * 32, 32), 32)
        pre_gate = f_gu[rows, 0:HID]
        pre_up = f_gu[rows, HID : 2 * HID]
        sig = jax.nn.sigmoid(pre_gate)
        act = pre_gate * sig
        hidden = (act * pre_up).astype(BF)
        hid[rows, :] = hidden
        scaled[rows, :] = (hidden.astype(F32) * factor_rows(rows)).astype(BF)
        f_gu[rows, 0:HID] = pre_up * sig * (1.0 + pre_gate * (1.0 - sig))
        f_gu[rows, HID : 2 * HID] = act
        return carry

    lax.fori_loop(0, ROWS // 32, first_part, 0)

    def dest(i):
        sign = 2 * (i % 2) - 1
        return lax.rem(y + 2 * NY + sign * (4 - (i + 1) // 2), NY)

    def order_of(direction, hop):
        if hop == 4:
            return 0
        return 7 - 2 * hop if direction == UP else 8 - 2 * hop

    def down_partial(i, carry):
        t = dest(i)
        part = dot_lead(rct[:, cols_of(t)], scaled[...]).astype(BF)
        p_down[t, 0] = part[:SHARD]
        p_down[t, 1] = part[SHARD:]
        return carry

    def y_copy(stream, direction, turn, src):
        return pltpu.make_async_remote_copy(
            src_ref=src,
            dst_ref=y_recv.at[stream, direction, turn],
            send_sem=ys_sem.at[stream, direction, turn],
            recv_sem=yr_sem.at[stream, direction, turn],
            device_id=y_dev[direction],
            device_id_type=MESH,
        )

    y_copies = {}

    def y_send(stream, direction, turn, src):
        copy = y_copy(stream, direction, turn, src)
        copy.start()
        y_copies[stream, direction, turn] = copy

    def own(stream, direction, hop):
        i = order_of(direction, hop)
        t = dest(i)
        if stream < 2:
            return p_down[t, other if stream == 0 else half].astype(F32)
        return p_gu[t, stream - 2].astype(F32)

    def first_turn(stream, direction):
        t = dest(order_of(direction, HOPS[stream, direction]))
        if stream < 2:
            y_send(stream, direction, 0, p_down.at[t, other if stream == 0 else half])
        else:
            y_send(stream, direction, 0, p_gu.at[t, stream - 2])

    def forward_turn(stream, direction, turn):
        y_copies[stream, direction, turn - 1].wait_recv()
        slot = y_recv.at[stream, direction, turn - 1]
        slot[...] = (slot[...].astype(F32) + own(stream, direction, HOPS[stream, direction] - turn)).astype(BF)
        y_send(stream, direction, turn, slot)

    def last_sum(stream):
        total = own(stream, UP, 0)
        for direction in (DOWN, UP):
            turn = HOPS[stream, direction] - 1
            y_copies[stream, direction, turn].wait_recv()
            total = total + y_recv[stream, direction, turn].astype(F32)
        return total

    lax.fori_loop(0, 3, down_partial, 0)
    for stream, direction in ((0, DOWN), (1, UP), (0, UP), (1, DOWN)):
        first_turn(stream, direction)
    lax.fori_loop(3, NY, down_partial, 0)

    loads[4].wait()
    f_back[...] = jnp.dot(rct[...], wd[...], preferred_element_type=F32)

    def second_part(i, carry):
        rows = pl.ds(pl.multiple_of(i * 32, 32), 32)
        back = f_back[rows, :]
        d_hidden = back * factor_rows(rows)
        dpre[rows, 0:HID] = (d_hidden * f_gu[rows, 0:HID]).astype(BF)
        dpre[rows, HID : 2 * HID] = (d_hidden * f_gu[rows, HID : 2 * HID]).astype(BF)
        f_back[rows, :] = hid[rows, :].astype(F32) * back
        return carry

    lax.fori_loop(0, ROWS // 32, second_part, 0)

    dpre_copy = plain_copy(dpre, dpre_x, xs_sem.at[1], xr_sem.at[1], x_dev)

    def gu_partial(i, carry):
        t = dest(i)
        part = (
            jnp.dot(rows_t[t, half], dpre[...], preferred_element_type=F32)
            + jnp.dot(rows_x[t], dpre_x[...], preferred_element_type=F32)
        ).astype(BF)
        p_gu[t, 0] = part[:, 0:HID]
        p_gu[t, 1] = part[:, HID : 2 * HID]
        return carry

    def dx_part(q, carry):
        rows = pl.ds(pl.multiple_of(q * 8 * FEAT, 8 * FEAT), 8 * FEAT)
        part = dot_last(wgu[rows, :], dpre[...]).astype(BF)
        for m in range(8):
            dx_own[(m // 2) % 2, 4 * q + 2 * (m // 4) + m % 2] = part[m * FEAT : (m + 1) * FEAT]
        return carry

    lax.fori_loop(0, D // (8 * FEAT), dx_part, 0)
    folded = f_back[:, 0:128] + f_back[:, 128:256] + f_back[:, 256:384]
    dots = jnp.sum(folded.T, axis=0, keepdims=True)
    dt_own[...] = jnp.broadcast_to(dots, (8, ROWS))

    dx_core_copy = plain_copy(dx_own.at[lax.rem(xl + 1 + colour, 2)], dx_core, cs_sem.at[0], cr_sem.at[0], core_dev)
    dt_core_copy = plain_copy(dt_own, dt_core, cs_sem.at[1], cr_sem.at[1], core_dev)

    rows_copy.wait_recv()
    theirs = rows_x.at[mine]
    pass_copy = plain_copy(theirs, theirs, xs_sem.at[2], xr_sem.at[2], core_dev)

    for stream, direction in ((0, DOWN), (1, UP), (0, UP), (1, DOWN)):
        forward_turn(stream, direction, 1)

    def remote(src, dst, send, recv, device):
        return pltpu.make_async_remote_copy(
            src_ref=src, dst_ref=dst, send_sem=send, recv_sem=recv, device_id=device, device_id_type=MESH
        )

    def dx_xl_copy():
        return remote(dx_core, dx_xl, cs_sem.at[2], cr_sem.at[2], xl_dev)

    def dt_xl_copy():
        return remote(dt_sum, dt_xl, cs_sem.at[3], cr_sem.at[3], xl_dev)

    def z_copy(step):
        target = lax.rem(z + step, NZ)
        return remote(
            dx_core.at[pl.ds(2 * target, 2)], dx_z.at[step], zs_sem.at[0, step], zr_sem.at[0, step], z_dev(step)
        )

    def z_dot_copy(step):
        return remote(dt_z.at[0], dt_z.at[step], zs_sem.at[1, step], zr_sem.at[1, step], z_dev(step))

    def dx_out_copy():
        return remote(dx_out, dx_fin, cs_sem.at[4], cr_sem.at[4], core_dev)

    def dt_out_copy():
        return remote(dt_fin, dt_out, cs_sem.at[5], cr_sem.at[5], core_dev)

    dx_core_copy.wait_recv()
    dt_core_copy.wait_recv()
    dt_sum[...] = dt_own[...] + dt_core[...]

    @pl.when(colour == 1)
    def _():
        def add_core(i, carry):
            dx_core[i] = (dx_core[i].astype(F32) + dx_own[1 - xl, i].astype(F32)).astype(BF)
            return carry

        lax.fori_loop(0, 2 * NZ, add_core, 0)
        dx_xl_copy().start()
        dt_xl_copy().start()

    dpre_copy.wait_recv()
    pass_copy.wait_recv()
    lax.fori_loop(0, 3, gu_partial, 0)
    for stream, direction in ((2, DOWN), (3, UP), (2, UP), (3, DOWN)):
        first_turn(stream, direction)
    lax.fori_loop(3, NY, gu_partial, 0)

    for stream, direction in ((0, DOWN), (1, UP), (0, UP), (1, DOWN)):
        forward_turn(stream, direction, 2)

    @pl.when(colour == 0)
    def _():
        dx_xl_copy().wait_recv()
        dt_xl_copy().wait_recv()

        def add_four(i, carry):
            dx_core[i] = (
                dx_core[i].astype(F32) + dx_own[xl, i].astype(F32) + dx_xl[i].astype(F32)
            ).astype(BF)
            return carry

        lax.fori_loop(0, 2 * NZ, add_four, 0)
        dt_z[0] = dt_sum[...] + dt_xl[...]
        pl.semaphore_wait(barrier, NZ - 1)

        def z_start(step, carry):
            z_copy(step).start()
            z_dot_copy(step).start()
            return carry

        lax.fori_loop(1, NZ, z_start, 0)

    forward_turn(0, DOWN, 3)
    forward_turn(1, UP, 3)
    for stream, direction in ((2, DOWN), (3, UP), (2, UP), (3, DOWN)):
        forward_turn(stream, direction, 1)

    ax_send[...] = last_sum(0).astype(BF)
    ax_copy = plain_copy(ax_send, ax_recv, as_sem.at[0], as_sem.at[1], x_dev)

    for stream, direction in ((2, DOWN), (3, UP), (2, UP), (3, DOWN)):
        forward_turn(stream, direction, 2)

    forward_turn(2, DOWN, 3)
    forward_turn(3, UP, 3)
    @pl.when(colour == 0)
    def _():
        def z_wait(step, carry):
            z_copy(step).wait_recv()
            z_dot_copy(step).wait_recv()
            return carry

        lax.fori_loop(1, NZ, z_wait, 0)

        def z_sum(step, total):
            return total + dx_z[step].astype(F32)

        dx_sum = lax.fori_loop(1, NZ, z_sum, dx_core[pl.ds(2 * z, 2)].astype(F32))
        f_back[0:FEAT, 0:ROWS] = dx_sum[0]
        f_back[FEAT : 2 * FEAT, 0:ROWS] = dx_sum[1]
        dx_out[...] = f_back[pl.ds(pl.multiple_of((1 - core) * FEAT, FEAT), FEAT), 0:ROWS].astype(BF)
        dx_fin[...] = f_back[pl.ds(pl.multiple_of(core * FEAT, FEAT), FEAT), 0:ROWS].astype(BF)
        dots = dt_z[z]
        for source in range(1, NZ):
            dots = dots + dt_z[lax.rem(z + NZ - source, NZ)]
        dt_fin[...] = dots
        dt_out[...] = dots
        dx_out_copy().start()
        dt_out_copy().start()

    down_sum = last_sum(1)
    ax_copy.wait_recv()
    gd_out[...] = (down_sum + ax_recv[...].astype(F32)).astype(BF)
    gg_out[...] = last_sum(2).astype(BF)
    gu_out[...] = last_sum(3).astype(BF)

    @pl.when(colour == 1)
    def _():
        dx_out_copy().wait_recv()
        dt_out_copy().wait_recv()

    grads = dx_fin[...].astype(F32)
    dots = dt_out[0:1, :]
    for j in range(3):
        block_cols = slice(j * BLOCK, (j + 1) * BLOCK)
        gtok_out[:, block_cols] = (
            grads[:, 0:BLOCK] * is_block[0][j] + grads[:, BLOCK:ROWS] * is_block[1][j]
        ).astype(BF)
        values = dots[:, 0:BLOCK] * (is_block[0][j] * live[0]) + dots[:, BLOCK:ROWS] * (is_block[1][j] * live[1])
        slots = slots_ref[:, block_cols]
        gprob_out[0:1, block_cols] = jnp.where(slots == 0, values, 0.0)
        gprob_out[1:2, block_cols] = jnp.where(slots == 1, values, 0.0)

    for copy in y_copies.values():
        copy.wait_send()
    for copy in (rows_copy, pass_copy, dpre_copy, dx_core_copy, dt_core_copy, ax_copy):
        copy.wait_send()

    @pl.when(colour == 1)
    def _():
        dx_xl_copy().wait_send()
        dt_xl_copy().wait_send()

    @pl.when(colour == 0)
    def _():
        def z_sent(step, carry):
            z_copy(step).wait_send()
            z_dot_copy(step).wait_send()
            return carry

        lax.fori_loop(1, NZ, z_sent, 0)
        dx_out_copy().wait_send()
        dt_out_copy().wait_send()


def finish(*refs):
    sem = refs[-1]
    count = len(refs) // 2
    copies = [pltpu.make_async_copy(refs[i], refs[count + i], sem.at[i]) for i in range(count)]
    for copy in copies:
        copy.start()
    for copy in copies:
        copy.wait()


def body(tokens, cotangent, w_gate, w_up, w_down_t, gate_probs, slot_ids, block_list, block_count):
    smem = pl.BlockSpec(memory_space=pltpu.SMEM)
    vmem = pl.BlockSpec(memory_space=pltpu.VMEM)
    anywhere = pl.BlockSpec(memory_space=pl.ANY)
    dma = pltpu.SemaphoreType.DMA
    shard = (SHARD, HID)
    partial = pl.pallas_call(
        kernel,
        out_shape=(
            jax.ShapeDtypeStruct((FEAT, TOK), BF),
            jax.ShapeDtypeStruct((2, TOK), F32),
            jax.ShapeDtypeStruct(shard, BF),
            jax.ShapeDtypeStruct(shard, BF),
            jax.ShapeDtypeStruct(shard, BF),
        ),
        in_specs=[smem, smem, vmem, vmem] + [anywhere] * 5,
        out_specs=(vmem,) * 5,
        scratch_shapes=[
            pltpu.VMEM((TOK, D), BF),
            pltpu.VMEM((TOK, D), BF),
            pltpu.VMEM((D, 2 * HID), BF),
            pltpu.VMEM((D, HID), BF),
            pltpu.VMEM((ROWS, D), BF),
            pltpu.VMEM((ROWS, D), BF),
            pltpu.VMEM((ROWS, 2 * HID), F32),
            pltpu.VMEM((ROWS, HID), F32),
            pltpu.VMEM((ROWS, HID), BF),
            pltpu.VMEM((ROWS, HID), BF),
            pltpu.VMEM((ROWS, 2 * HID), BF),
            pltpu.VMEM((ROWS, BLOCK), F32),
            pltpu.VMEM((2, 3, 16, 128), BF),
            pltpu.VMEM((NY, 2, SHARD, ROWS), BF),
            pltpu.VMEM((NY, SHARD, ROWS), BF),
            pltpu.VMEM((ROWS, 2 * HID), BF),
            pltpu.VMEM((NY, 2) + shard, BF),
            pltpu.VMEM((NY, 2) + shard, BF),
            pltpu.VMEM((4, 2, 4) + shard, BF),
            pltpu.VMEM(shard, BF),
            pltpu.VMEM(shard, BF),
            pltpu.VMEM((2, 2 * NZ, FEAT, ROWS), BF),
            pltpu.VMEM((2 * NZ, FEAT, ROWS), BF),
            pltpu.VMEM((2 * NZ, FEAT, ROWS), BF),
            pltpu.VMEM((NZ, 2, FEAT, ROWS), BF),
            pltpu.VMEM((FEAT, ROWS), BF),
            pltpu.VMEM((FEAT, ROWS), BF),
            pltpu.VMEM((8, ROWS), F32),
            pltpu.VMEM((8, ROWS), F32),
            pltpu.VMEM((8, ROWS), F32),
            pltpu.VMEM((8, ROWS), F32),
            pltpu.VMEM((NZ, 8, ROWS), F32),
            pltpu.VMEM((8, ROWS), F32),
            pltpu.VMEM((8, ROWS), F32),
            dma((5,)),
            dma((3,)),
            dma((3,)),
            dma((4, 2, 4)),
            dma((4, 2, 4)),
            dma((2,)),
            dma((6,)),
            dma((6,)),
            dma((2, NZ)),
            dma((2, NZ)),
            pltpu.SemaphoreType.REGULAR,
        ],
        compiler_params=pltpu.CompilerParams(
            collective_id=0, has_side_effects=True, vmem_limit_bytes=52 * 1024 * 1024
        ),
        name="expert_backward",
    )(
        block_list, block_count, gate_probs.T, slot_ids.reshape(1, TOK),
        tokens, cotangent, w_gate, w_up, w_down_t,
    )
    gtok, gprob, gg, gu, gd = pl.pallas_call(
        finish,
        out_shape=tuple(jax.ShapeDtypeStruct(part.shape, part.dtype) for part in partial),
        in_specs=[anywhere] * 5,
        out_specs=(anywhere,) * 5,
        scratch_shapes=[dma((5,))],
        name="finish",
    )(*partial)
    return gtok.T, gprob.T, gg, gu, gd


def solution(mesh):
    placed = (
        P("dp", None),
        P("dp", None),
        P(None, "blk"),
        P(None, "blk"),
        P(None, "blk"),
        P("dp", None),
        P("dp"),
        P("dp", None),
        P("dp"),
    )
    return jax.shard_map(
        body,
        mesh=mesh,
        in_specs=placed,
        out_specs=(P("dp", "blk"), P("dp", None), P("dp", "blk"), P("dp", "blk"), P("dp", "blk")),
        check_vma=False,
    )
```

```python
import jax
import jax.numpy as jnp
from jax import lax
from jax.experimental import pallas as pl
from jax.experimental.pallas import tpu as pltpu
from jax.sharding import PartitionSpec as P

MESH = pl.DeviceIdType.MESH
BF = jnp.bfloat16
F32 = jnp.float32

D = 3072
HID = 384
BLOCK = 128
TOK = 384
ROWS = 256
NY = 8
NZ = 12
SHARD = 192
FEAT = 64
CHUNK = 384
PARTS = 4

DOWN, UP = 0, 1
HOPS = {(0, DOWN): 4, (0, UP): 3, (1, DOWN): 3, (1, UP): 4, (2, DOWN): 4, (2, UP): 3, (3, DOWN): 3, (3, UP): 4}


def dot_lead(left, right):
    return lax.dot_general(left, right, (((0,), (0,)), ((), ())), preferred_element_type=F32)


def dot_last(left, right):
    return lax.dot_general(left, right, (((1,), (1,)), ((), ())), preferred_element_type=F32)


def kernel(
    list_ref, count_ref, probs_ref, slots_ref, tok_hbm, cot_hbm, wg_hbm, wu_hbm, wd_hbm,
    gtok_out, gprob_out, gg_out, gu_out, gd_out,
    tok, cot, wgu, wd, rin, rct, f_gu, f_back, hid, scaled, dpre, fac, picks,
    rows_t, rows_x, dpre_x, p_down, p_gu, y_recv, ax_send, ax_recv,
    dx_own, dx_core, dx_xl, dx_z, dx_out, dx_fin, dt_own, dt_core, dt_sum, dt_xl, dt_z, dt_out, dt_fin,
    load_sem, xs_sem, xr_sem, ys_sem, yr_sem, as_sem, cs_sem, cr_sem, zs_sem, zr_sem, ready,
):
    blk = lax.axis_index("blk")
    dp = lax.axis_index("dp")
    z = blk // 4
    xl = lax.rem(blk // 2, 2)
    core = lax.rem(blk, 2)
    y = dp // 2
    half = lax.rem(dp, 2)
    other = 1 - half
    colour = lax.rem(y + half + xl + core, 2)

    def at(zz=None, xx=None, cc=None):
        zz = z if zz is None else zz
        xx = xl if xx is None else xx
        cc = core if cc is None else cc
        return (zz * 4 + xx * 2 + cc, dp)

    y_dev = {
        DOWN: (blk, lax.rem(y + NY - 1, NY) * 2 + half),
        UP: (blk, lax.rem(y + 1, NY) * 2 + half),
    }
    x_dev = (blk, y * 2 + other)
    core_dev = at(cc=1 - core)
    xl_dev = at(xx=1 - xl)

    def z_dev(step):
        return at(zz=lax.rem(z + step, NZ))

    part_rows = D // PARTS
    sources = [(tok_hbm, tok), (cot_hbm, cot)]
    for k in range(PARTS):
        rows = pl.ds(k * part_rows, part_rows)
        sources.append((wg_hbm.at[rows], wgu.at[rows, 0:HID]))
        sources.append((wu_hbm.at[rows], wgu.at[rows, HID : 2 * HID]))
    sources.append((wd_hbm, wd))
    loads = [pltpu.make_async_copy(src, dst, load_sem.at[i]) for i, (src, dst) in enumerate(sources)]
    for load in loads:
        load.start()

    plane = (y_dev[DOWN], y_dev[UP], x_dev, core_dev, xl_dev)
    barrier = pltpu.get_barrier_semaphore()

    @pl.when(colour == 0)
    def _():
        for partner in plane:
            pl.semaphore_signal(barrier, inc=1, device_id=partner, device_id_type=MESH)
        for step in range(1, NZ):
            pl.semaphore_signal(barrier, inc=1, device_id=z_dev(step), device_id_type=MESH)

    blocks = [list_ref[0, k] for k in range(2)]
    live = [(count_ref[0] > k).astype(F32) for k in range(2)]
    is_block = [[(block == j).astype(F32) for j in range(3)] for block in blocks]

    gates_row = jnp.where(slots_ref[...] == 0, probs_ref[0:1, :], probs_ref[1:2, :])
    diagonal = lax.broadcasted_iota(jnp.int32, (BLOCK, BLOCK), 0) == lax.broadcasted_iota(
        jnp.int32, (BLOCK, BLOCK), 1
    )
    columns = [
        jnp.sum(jnp.where(diagonal, gates_row[:, j * BLOCK : (j + 1) * BLOCK], 0.0), axis=1, keepdims=True)
        for j in range(3)
    ]
    for k in range(2):
        column = sum(columns[j] * is_block[k][j] for j in range(3))
        fac[k * BLOCK : (k + 1) * BLOCK, :] = jnp.broadcast_to(column * live[k], (BLOCK, BLOCK))
        for j in range(3):
            picks[k, j] = jnp.broadcast_to(is_block[k][j], (16, 128)).astype(BF)

    def take_rows(source, target):
        def step(i, carry):
            for col in range(0, D, 128):
                parts = [source[pl.ds(pl.multiple_of(j * BLOCK + i * 16, 16), 16), col : col + 128] for j in range(3)]
                for k in range(2):
                    target[pl.ds(pl.multiple_of(k * BLOCK + i * 16, 16), 16), col : col + 128] = (
                        parts[0] * picks[k, 0] + parts[1] * picks[k, 1] + parts[2] * picks[k, 2]
                    )
            return carry

        lax.fori_loop(0, BLOCK // 16, step, 0)

    loads[0].wait()
    take_rows(tok, rin)

    @pl.when(colour == 1)
    def _():
        pl.semaphore_wait(barrier, len(plane))
        for partner in plane:
            pl.semaphore_signal(ready, inc=1, device_id=partner, device_id_type=MESH)

    def cols_of(t):
        return pl.ds(pl.multiple_of(t * CHUNK, CHUNK), CHUNK)

    def turn_rows(t, carry):
        part = rin[:, cols_of(t)].T
        rows_t[t, 0] = part[:SHARD]
        rows_t[t, 1] = part[SHARD:]
        return carry

    def plain_copy(src, dst, send, recv, device):
        copy = pltpu.make_async_remote_copy(
            src_ref=src, dst_ref=dst, send_sem=send, recv_sem=recv, device_id=device, device_id_type=MESH
        )
        copy.start()
        return copy

    lax.fori_loop(0, NY, turn_rows, 0)
    @pl.when(colour == 0)
    def _():
        pl.semaphore_wait(ready, len(plane))

    mine = pl.ds((NY // 2) * core, NY // 2)
    rows_copy = plain_copy(rows_t.at[mine, other], rows_x.at[mine], xs_sem.at[0], xr_sem.at[0], x_dev)

    loads[1].wait()
    take_rows(cot, rct)
    for k in range(PARTS):
        loads[2 + 2 * k].wait()
        loads[3 + 2 * k].wait()
        rows = slice(k * part_rows, (k + 1) * part_rows)
        product = jnp.dot(rin[:, rows], wgu[rows, :], preferred_element_type=F32)
        f_gu[...] = product if k == 0 else f_gu[...] + product

    def factor_rows(rows):
        column = fac[rows, :]
        return jnp.concatenate([column, column, column], axis=1)

    def first_part(i, carry):
        rows = pl.ds(pl.multiple_of(i * 32, 32), 32)
        pre_gate = f_gu[rows, 0:HID]
        pre_up = f_gu[rows, HID : 2 * HID]
        sig = jax.nn.sigmoid(pre_gate)
        act = pre_gate * sig
        hidden = (act * pre_up).astype(BF)
        hid[rows, :] = hidden
        scaled[rows, :] = (hidden.astype(F32) * factor_rows(rows)).astype(BF)
        f_gu[rows, 0:HID] = pre_up * sig * (1.0 + pre_gate * (1.0 - sig))
        f_gu[rows, HID : 2 * HID] = act
        return carry

    lax.fori_loop(0, ROWS // 32, first_part, 0)

    def dest(i):
        sign = 2 * (i % 2) - 1
        return lax.rem(y + 2 * NY + sign * (4 - (i + 1) // 2), NY)

    def order_of(direction, hop):
        if hop == 4:
            return 0
        return 7 - 2 * hop if direction == UP else 8 - 2 * hop

    def down_partial(i, carry):
        t = dest(i)
        part = dot_lead(rct[:, cols_of(t)], scaled[...]).astype(BF)
        p_down[t, 0] = part[:SHARD]
        p_down[t, 1] = part[SHARD:]
        return carry

    def y_copy(stream, direction, turn, src):
        return pltpu.make_async_remote_copy(
            src_ref=src,
            dst_ref=y_recv.at[stream, direction, turn],
            send_sem=ys_sem.at[stream, direction, turn],
            recv_sem=yr_sem.at[stream, direction, turn],
            device_id=y_dev[direction],
            device_id_type=MESH,
        )

    y_copies = {}

    def y_send(stream, direction, turn, src):
        copy = y_copy(stream, direction, turn, src)
        copy.start()
        y_copies[stream, direction, turn] = copy

    def own(stream, direction, hop):
        i = order_of(direction, hop)
        t = dest(i)
        if stream < 2:
            return p_down[t, other if stream == 0 else half].astype(F32)
        return p_gu[t, stream - 2].astype(F32)

    def first_turn(stream, direction):
        t = dest(order_of(direction, HOPS[stream, direction]))
        if stream < 2:
            y_send(stream, direction, 0, p_down.at[t, other if stream == 0 else half])
        else:
            y_send(stream, direction, 0, p_gu.at[t, stream - 2])

    def forward_turn(stream, direction, turn):
        y_copies[stream, direction, turn - 1].wait_recv()
        slot = y_recv.at[stream, direction, turn - 1]
        slot[...] = (slot[...].astype(F32) + own(stream, direction, HOPS[stream, direction] - turn)).astype(BF)
        y_send(stream, direction, turn, slot)

    def last_sum(stream):
        total = own(stream, UP, 0)
        for direction in (DOWN, UP):
            turn = HOPS[stream, direction] - 1
            y_copies[stream, direction, turn].wait_recv()
            total = total + y_recv[stream, direction, turn].astype(F32)
        return total

    down_partial(0, 0)

    first_turn(0, DOWN)
    first_turn(1, UP)
    lax.fori_loop(1, 3, down_partial, 0)
    first_turn(0, UP)
    first_turn(1, DOWN)

    loads[2 + 2 * PARTS].wait()
    f_back[...] = jnp.dot(rct[...], wd[...], preferred_element_type=F32)

    def second_part(i, carry):
        rows = pl.ds(pl.multiple_of(i * 32, 32), 32)
        back = f_back[rows, :]
        d_hidden = back * factor_rows(rows)
        dpre[rows, 0:HID] = (d_hidden * f_gu[rows, 0:HID]).astype(BF)
        dpre[rows, HID : 2 * HID] = (d_hidden * f_gu[rows, HID : 2 * HID]).astype(BF)
        f_back[rows, :] = hid[rows, :].astype(F32) * back
        return carry

    lax.fori_loop(0, ROWS // 32, second_part, 0)

    dpre_copy = plain_copy(dpre, dpre_x, xs_sem.at[1], xr_sem.at[1], x_dev)
    lax.fori_loop(3, NY, down_partial, 0)

    def gu_partial(i, carry):
        t = dest(i)
        part = (
            jnp.dot(rows_t[t, half], dpre[...], preferred_element_type=F32)
            + jnp.dot(rows_x[t], dpre_x[...], preferred_element_type=F32)
        ).astype(BF)
        p_gu[t, 0] = part[:, 0:HID]
        p_gu[t, 1] = part[:, HID : 2 * HID]
        return carry

    def dx_part(q, carry):
        rows = pl.ds(pl.multiple_of(q * 8 * FEAT, 8 * FEAT), 8 * FEAT)
        part = dot_last(wgu[rows, :], dpre[...]).astype(BF)
        for m in range(8):
            dx_own[(m // 2) % 2, 4 * q + 2 * (m // 4) + m % 2] = part[m * FEAT : (m + 1) * FEAT]
        return carry

    lax.fori_loop(0, D // (8 * FEAT), dx_part, 0)
    folded = f_back[:, 0:128] + f_back[:, 128:256] + f_back[:, 256:384]
    dots = jnp.sum(folded.T, axis=0, keepdims=True)
    dt_own[...] = jnp.broadcast_to(dots, (8, ROWS))

    dx_core_copy = plain_copy(dx_own.at[lax.rem(xl + 1 + colour, 2)], dx_core, cs_sem.at[0], cr_sem.at[0], core_dev)
    dt_core_copy = plain_copy(dt_own, dt_core, cs_sem.at[1], cr_sem.at[1], core_dev)

    rows_copy.wait_recv()
    theirs = rows_x.at[mine]
    pass_copy = plain_copy(theirs, theirs, xs_sem.at[2], xr_sem.at[2], core_dev)

    for stream, direction in ((0, DOWN), (1, UP), (0, UP), (1, DOWN)):
        forward_turn(stream, direction, 1)

    def remote(src, dst, send, recv, device):
        return pltpu.make_async_remote_copy(
            src_ref=src, dst_ref=dst, send_sem=send, recv_sem=recv, device_id=device, device_id_type=MESH
        )

    def dx_xl_copy():
        return remote(dx_core, dx_xl, cs_sem.at[2], cr_sem.at[2], xl_dev)

    def dt_xl_copy():
        return remote(dt_sum, dt_xl, cs_sem.at[3], cr_sem.at[3], xl_dev)

    def z_copy(step):
        target = lax.rem(z + step, NZ)
        return remote(
            dx_core.at[pl.ds(2 * target, 2)], dx_z.at[step], zs_sem.at[0, step], zr_sem.at[0, step], z_dev(step)
        )

    def z_dot_copy(step):
        return remote(dt_z.at[0], dt_z.at[step], zs_sem.at[1, step], zr_sem.at[1, step], z_dev(step))

    def dx_out_copy():
        return remote(dx_out, dx_fin, cs_sem.at[4], cr_sem.at[4], core_dev)

    def dt_out_copy():
        return remote(dt_fin, dt_out, cs_sem.at[5], cr_sem.at[5], core_dev)

    dx_core_copy.wait_recv()
    dt_core_copy.wait_recv()
    dt_sum[...] = dt_own[...] + dt_core[...]

    @pl.when(colour == 1)
    def _():
        def add_core(i, carry):
            dx_core[i] = (dx_core[i].astype(F32) + dx_own[1 - xl, i].astype(F32)).astype(BF)
            return carry

        lax.fori_loop(0, 2 * NZ, add_core, 0)
        dx_xl_copy().start()
        dt_xl_copy().start()

    for stream, direction in ((0, DOWN), (1, UP), (0, UP), (1, DOWN)):
        forward_turn(stream, direction, 2)
    dpre_copy.wait_recv()
    pass_copy.wait_recv()
    gu_partial(0, 0)
    first_turn(2, DOWN)
    first_turn(3, UP)
    lax.fori_loop(1, 3, gu_partial, 0)
    first_turn(2, UP)
    first_turn(3, DOWN)
    lax.fori_loop(3, NY, gu_partial, 0)


    @pl.when(colour == 0)
    def _():
        dx_xl_copy().wait_recv()
        dt_xl_copy().wait_recv()

        def add_four(i, carry):
            dx_core[i] = (
                dx_core[i].astype(F32) + dx_own[xl, i].astype(F32) + dx_xl[i].astype(F32)
            ).astype(BF)
            return carry

        lax.fori_loop(0, 2 * NZ, add_four, 0)
        dt_z[0] = dt_sum[...] + dt_xl[...]
        pl.semaphore_wait(barrier, NZ - 1)

        def z_start(step, carry):
            z_copy(step).start()
            z_dot_copy(step).start()
            return carry

        lax.fori_loop(1, NZ, z_start, 0)

    forward_turn(0, DOWN, 3)
    forward_turn(1, UP, 3)
    for stream, direction in ((2, DOWN), (3, UP), (2, UP), (3, DOWN)):
        forward_turn(stream, direction, 1)

    ax_send[...] = last_sum(0).astype(BF)
    ax_copy = plain_copy(ax_send, ax_recv, as_sem.at[0], as_sem.at[1], x_dev)

    for stream, direction in ((2, DOWN), (3, UP), (2, UP), (3, DOWN)):
        forward_turn(stream, direction, 2)

    forward_turn(2, DOWN, 3)
    forward_turn(3, UP, 3)
    @pl.when(colour == 0)
    def _():
        def z_wait(step, carry):
            z_copy(step).wait_recv()
            z_dot_copy(step).wait_recv()
            return carry

        lax.fori_loop(1, NZ, z_wait, 0)

        def z_sum(step, total):
            return total + dx_z[step].astype(F32)

        dx_sum = lax.fori_loop(1, NZ, z_sum, dx_core[pl.ds(2 * z, 2)].astype(F32))
        f_back[0:FEAT, 0:ROWS] = dx_sum[0]
        f_back[FEAT : 2 * FEAT, 0:ROWS] = dx_sum[1]
        dx_out[...] = f_back[pl.ds(pl.multiple_of((1 - core) * FEAT, FEAT), FEAT), 0:ROWS].astype(BF)
        dx_fin[...] = f_back[pl.ds(pl.multiple_of(core * FEAT, FEAT), FEAT), 0:ROWS].astype(BF)
        dots = dt_z[z]
        for source in range(1, NZ):
            dots = dots + dt_z[lax.rem(z + NZ - source, NZ)]
        dt_fin[...] = dots
        dt_out[...] = dots
        dx_out_copy().start()
        dt_out_copy().start()

    down_sum = last_sum(1)
    ax_copy.wait_recv()
    gd_out[...] = (down_sum + ax_recv[...].astype(F32)).astype(BF)
    gg_out[...] = last_sum(2).astype(BF)
    gu_out[...] = last_sum(3).astype(BF)

    @pl.when(colour == 1)
    def _():
        dx_out_copy().wait_recv()
        dt_out_copy().wait_recv()

    grads = dx_fin[...].astype(F32)
    dots = dt_out[0:1, :]
    for j in range(3):
        block_cols = slice(j * BLOCK, (j + 1) * BLOCK)
        gtok_out[:, block_cols] = (
            grads[:, 0:BLOCK] * is_block[0][j] + grads[:, BLOCK:ROWS] * is_block[1][j]
        ).astype(BF)
        values = dots[:, 0:BLOCK] * (is_block[0][j] * live[0]) + dots[:, BLOCK:ROWS] * (is_block[1][j] * live[1])
        slots = slots_ref[:, block_cols]
        gprob_out[0:1, block_cols] = jnp.where(slots == 0, values, 0.0)
        gprob_out[1:2, block_cols] = jnp.where(slots == 1, values, 0.0)

    for copy in y_copies.values():
        copy.wait_send()
    for copy in (rows_copy, pass_copy, dpre_copy, dx_core_copy, dt_core_copy, ax_copy):
        copy.wait_send()

    @pl.when(colour == 1)
    def _():
        dx_xl_copy().wait_send()
        dt_xl_copy().wait_send()

    @pl.when(colour == 0)
    def _():
        def z_sent(step, carry):
            z_copy(step).wait_send()
            z_dot_copy(step).wait_send()
            return carry

        lax.fori_loop(1, NZ, z_sent, 0)
        dx_out_copy().wait_send()
        dt_out_copy().wait_send()


def body(tokens, cotangent, w_gate, w_up, w_down_t, gate_probs, slot_ids, block_list, block_count):
    smem = pl.BlockSpec(memory_space=pltpu.SMEM)
    vmem = pl.BlockSpec(memory_space=pltpu.VMEM)
    anywhere = pl.BlockSpec(memory_space=pl.ANY)
    dma = pltpu.SemaphoreType.DMA
    shard = (SHARD, HID)
    gtok, gprob, gg, gu, gd = pl.pallas_call(
        kernel,
        out_shape=(
            jax.ShapeDtypeStruct((FEAT, TOK), BF),
            jax.ShapeDtypeStruct((2, TOK), F32),
            jax.ShapeDtypeStruct(shard, BF),
            jax.ShapeDtypeStruct(shard, BF),
            jax.ShapeDtypeStruct(shard, BF),
        ),
        in_specs=[smem, smem, vmem, vmem] + [anywhere] * 5,
        out_specs=(vmem,) * 5,
        scratch_shapes=[
            pltpu.VMEM((TOK, D), BF),
            pltpu.VMEM((TOK, D), BF),
            pltpu.VMEM((D, 2 * HID), BF),
            pltpu.VMEM((D, HID), BF),
            pltpu.VMEM((ROWS, D), BF),
            pltpu.VMEM((ROWS, D), BF),
            pltpu.VMEM((ROWS, 2 * HID), F32),
            pltpu.VMEM((ROWS, HID), F32),
            pltpu.VMEM((ROWS, HID), BF),
            pltpu.VMEM((ROWS, HID), BF),
            pltpu.VMEM((ROWS, 2 * HID), BF),
            pltpu.VMEM((ROWS, BLOCK), F32),
            pltpu.VMEM((2, 3, 16, 128), BF),
            pltpu.VMEM((NY, 2, SHARD, ROWS), BF),
            pltpu.VMEM((NY, SHARD, ROWS), BF),
            pltpu.VMEM((ROWS, 2 * HID), BF),
            pltpu.VMEM((NY, 2) + shard, BF),
            pltpu.VMEM((NY, 2) + shard, BF),
            pltpu.VMEM((4, 2, 4) + shard, BF),
            pltpu.VMEM(shard, BF),
            pltpu.VMEM(shard, BF),
            pltpu.VMEM((2, 2 * NZ, FEAT, ROWS), BF),
            pltpu.VMEM((2 * NZ, FEAT, ROWS), BF),
            pltpu.VMEM((2 * NZ, FEAT, ROWS), BF),
            pltpu.VMEM((NZ, 2, FEAT, ROWS), BF),
            pltpu.VMEM((FEAT, ROWS), BF),
            pltpu.VMEM((FEAT, ROWS), BF),
            pltpu.VMEM((8, ROWS), F32),
            pltpu.VMEM((8, ROWS), F32),
            pltpu.VMEM((8, ROWS), F32),
            pltpu.VMEM((8, ROWS), F32),
            pltpu.VMEM((NZ, 8, ROWS), F32),
            pltpu.VMEM((8, ROWS), F32),
            pltpu.VMEM((8, ROWS), F32),
            dma((2 * PARTS + 3,)),
            dma((3,)),
            dma((3,)),
            dma((4, 2, 4)),
            dma((4, 2, 4)),
            dma((2,)),
            dma((6,)),
            dma((6,)),
            dma((2, NZ)),
            dma((2, NZ)),
            pltpu.SemaphoreType.REGULAR,
        ],
        compiler_params=pltpu.CompilerParams(
            collective_id=0, has_side_effects=True, vmem_limit_bytes=52 * 1024 * 1024
        ),
        name="expert_backward",
    )(
        block_list, block_count, gate_probs.T, slot_ids.reshape(1, TOK),
        tokens, cotangent, w_gate, w_up, w_down_t,
    )
    return gtok.T, gprob.T, gg, gu, gd


def solution(mesh):
    placed = (
        P("dp", None),
        P("dp", None),
        P(None, "blk"),
        P(None, "blk"),
        P(None, "blk"),
        P("dp", None),
        P("dp"),
        P("dp", None),
        P("dp"),
    )
    return jax.shard_map(
        body,
        mesh=mesh,
        in_specs=placed,
        out_specs=(P("dp", "blk"), P("dp", None), P("dp", "blk"), P("dp", "blk"), P("dp", "blk")),
        check_vma=False,
    )
```

```python
import jax
import jax.numpy as jnp
from jax import lax
from jax.experimental import pallas as pl
from jax.experimental.pallas import tpu as pltpu
from jax.sharding import PartitionSpec as P

MESH = pl.DeviceIdType.MESH
BF = jnp.bfloat16
F32 = jnp.float32

D = 3072
HID = 384
BLOCK = 128
TOK = 384
ROWS = 256
NY = 8
NZ = 12
SHARD = 192
FEAT = 64
CHUNK = 384
PARTS = 4

DOWN, UP = 0, 1
HOPS = {(0, DOWN): 4, (0, UP): 3, (1, DOWN): 3, (1, UP): 4, (2, DOWN): 4, (2, UP): 3, (3, DOWN): 3, (3, UP): 4}


def dot_lead(left, right):
    return lax.dot_general(left, right, (((0,), (0,)), ((), ())), preferred_element_type=F32)


def dot_last(left, right):
    return lax.dot_general(left, right, (((1,), (1,)), ((), ())), preferred_element_type=F32)


def kernel(
    list_ref, count_ref, probs_ref, slots_ref, tok_hbm, cot_hbm, wg_hbm, wu_hbm, wd_hbm,
    gtok_out, gprob_out, gg_out, gu_out, gd_out,
    tok, cot, wgu, wd, rin, rct, f_gu, f_back, hid, scaled, dpre, fac, picks,
    rows_t, rows_x, dpre_x, p_down, p_gu, y_recv, ax_send, ax_recv,
    dx_own, dx_core, dx_xl, dx_z, dx_out, dx_fin, dt_own, dt_core, dt_sum, dt_xl, dt_z, dt_out, dt_fin,
    load_sem, xs_sem, xr_sem, ys_sem, yr_sem, as_sem, cs_sem, cr_sem, zs_sem, zr_sem, ready,
):
    blk = lax.axis_index("blk")
    dp = lax.axis_index("dp")
    z = blk // 4
    xl = lax.rem(blk // 2, 2)
    core = lax.rem(blk, 2)
    y = dp // 2
    half = lax.rem(dp, 2)
    other = 1 - half
    colour = lax.rem(y + half + xl + core, 2)

    def at(zz=None, xx=None, cc=None):
        zz = z if zz is None else zz
        xx = xl if xx is None else xx
        cc = core if cc is None else cc
        return (zz * 4 + xx * 2 + cc, dp)

    y_dev = {
        DOWN: (blk, lax.rem(y + NY - 1, NY) * 2 + half),
        UP: (blk, lax.rem(y + 1, NY) * 2 + half),
    }
    x_dev = (blk, y * 2 + other)
    core_dev = at(cc=1 - core)
    xl_dev = at(xx=1 - xl)

    def z_dev(step):
        return at(zz=lax.rem(z + step, NZ))

    part_rows = D // PARTS
    sources = [(tok_hbm, tok), (cot_hbm, cot)]
    for k in range(PARTS):
        rows = pl.ds(k * part_rows, part_rows)
        sources.append((wg_hbm.at[rows], wgu.at[rows, 0:HID]))
        sources.append((wu_hbm.at[rows], wgu.at[rows, HID : 2 * HID]))
    sources.append((wd_hbm, wd))
    loads = [pltpu.make_async_copy(src, dst, load_sem.at[i]) for i, (src, dst) in enumerate(sources)]
    for load in loads:
        load.start()

    plane = (y_dev[DOWN], y_dev[UP], x_dev, core_dev, xl_dev)
    barrier = pltpu.get_barrier_semaphore()

    @pl.when(colour == 0)
    def _():
        for partner in plane:
            pl.semaphore_signal(barrier, inc=1, device_id=partner, device_id_type=MESH)
        for step in range(1, NZ):
            pl.semaphore_signal(barrier, inc=1, device_id=z_dev(step), device_id_type=MESH)

    blocks = [list_ref[0, k] for k in range(2)]
    live = [(count_ref[0] > k).astype(F32) for k in range(2)]
    is_block = [[(block == j).astype(F32) for j in range(3)] for block in blocks]

    gates_row = jnp.where(slots_ref[...] == 0, probs_ref[0:1, :], probs_ref[1:2, :])
    diagonal = lax.broadcasted_iota(jnp.int32, (BLOCK, BLOCK), 0) == lax.broadcasted_iota(
        jnp.int32, (BLOCK, BLOCK), 1
    )
    columns = [
        jnp.sum(jnp.where(diagonal, gates_row[:, j * BLOCK : (j + 1) * BLOCK], 0.0), axis=1, keepdims=True)
        for j in range(3)
    ]
    for k in range(2):
        column = sum(columns[j] * is_block[k][j] for j in range(3))
        fac[k * BLOCK : (k + 1) * BLOCK, :] = jnp.broadcast_to(column * live[k], (BLOCK, BLOCK))
        for j in range(3):
            picks[k, j] = jnp.broadcast_to(is_block[k][j], (16, 128)).astype(BF)

    def take_rows(source, target):
        def step(i, carry):
            for col in range(0, D, 128):
                parts = [source[pl.ds(pl.multiple_of(j * BLOCK + i * 16, 16), 16), col : col + 128] for j in range(3)]
                for k in range(2):
                    target[pl.ds(pl.multiple_of(k * BLOCK + i * 16, 16), 16), col : col + 128] = (
                        parts[0] * picks[k, 0] + parts[1] * picks[k, 1] + parts[2] * picks[k, 2]
                    )
            return carry

        lax.fori_loop(0, BLOCK // 16, step, 0)

    loads[0].wait()
    take_rows(tok, rin)

    @pl.when(colour == 1)
    def _():
        pl.semaphore_wait(barrier, len(plane))
        for partner in plane:
            pl.semaphore_signal(ready, inc=1, device_id=partner, device_id_type=MESH)

    def cols_of(t):
        return pl.ds(pl.multiple_of(t * CHUNK, CHUNK), CHUNK)

    def turn_rows(t, carry):
        part = rin[:, cols_of(t)].T
        rows_t[t, 0] = part[:SHARD]
        rows_t[t, 1] = part[SHARD:]
        return carry

    def plain_copy(src, dst, send, recv, device):
        copy = pltpu.make_async_remote_copy(
            src_ref=src, dst_ref=dst, send_sem=send, recv_sem=recv, device_id=device, device_id_type=MESH
        )
        copy.start()
        return copy

    first_half = (NY // 2) * core
    lax.fori_loop(first_half, first_half + NY // 2, turn_rows, 0)
    @pl.when(colour == 0)
    def _():
        pl.semaphore_wait(ready, len(plane))

    mine = pl.ds((NY // 2) * core, NY // 2)
    rows_copy = plain_copy(rows_t.at[mine, other], rows_x.at[mine], xs_sem.at[0], xr_sem.at[0], x_dev)

    loads[1].wait()
    take_rows(cot, rct)
    for k in range(PARTS):
        loads[2 + 2 * k].wait()
        loads[3 + 2 * k].wait()
        rows = slice(k * part_rows, (k + 1) * part_rows)
        product = jnp.dot(rin[:, rows], wgu[rows, :], preferred_element_type=F32)
        f_gu[...] = product if k == 0 else f_gu[...] + product

    def factor_rows(rows):
        column = fac[rows, :]
        return jnp.concatenate([column, column, column], axis=1)

    def first_part(i, carry):
        rows = pl.ds(pl.multiple_of(i * 32, 32), 32)
        pre_gate = f_gu[rows, 0:HID]
        pre_up = f_gu[rows, HID : 2 * HID]
        sig = jax.nn.sigmoid(pre_gate)
        act = pre_gate * sig
        hidden = (act * pre_up).astype(BF)
        hid[rows, :] = hidden
        scaled[rows, :] = (hidden.astype(F32) * factor_rows(rows)).astype(BF)
        f_gu[rows, 0:HID] = pre_up * sig * (1.0 + pre_gate * (1.0 - sig))
        f_gu[rows, HID : 2 * HID] = act
        return carry

    lax.fori_loop(0, ROWS // 32, first_part, 0)

    def dest(i):
        sign = 2 * (i % 2) - 1
        return lax.rem(y + 2 * NY + sign * (4 - (i + 1) // 2), NY)

    def order_of(direction, hop):
        if hop == 4:
            return 0
        return 7 - 2 * hop if direction == UP else 8 - 2 * hop

    def down_partial(i, carry):
        t = dest(i)
        part = dot_lead(rct[:, cols_of(t)], scaled[...]).astype(BF)
        p_down[t, 0] = part[:SHARD]
        p_down[t, 1] = part[SHARD:]
        return carry

    def y_copy(stream, direction, turn, src):
        return pltpu.make_async_remote_copy(
            src_ref=src,
            dst_ref=y_recv.at[stream, direction, turn],
            send_sem=ys_sem.at[stream, direction, turn],
            recv_sem=yr_sem.at[stream, direction, turn],
            device_id=y_dev[direction],
            device_id_type=MESH,
        )

    y_copies = {}

    def y_send(stream, direction, turn, src):
        copy = y_copy(stream, direction, turn, src)
        copy.start()
        y_copies[stream, direction, turn] = copy

    def own(stream, direction, hop):
        i = order_of(direction, hop)
        t = dest(i)
        if stream < 2:
            return p_down[t, other if stream == 0 else half].astype(F32)
        return p_gu[t, stream - 2].astype(F32)

    def first_turn(stream, direction):
        t = dest(order_of(direction, HOPS[stream, direction]))
        if stream < 2:
            y_send(stream, direction, 0, p_down.at[t, other if stream == 0 else half])
        else:
            y_send(stream, direction, 0, p_gu.at[t, stream - 2])

    def forward_turn(stream, direction, turn):
        y_copies[stream, direction, turn - 1].wait_recv()
        slot = y_recv.at[stream, direction, turn - 1]
        slot[...] = (slot[...].astype(F32) + own(stream, direction, HOPS[stream, direction] - turn)).astype(BF)
        y_send(stream, direction, turn, slot)

    def last_sum(stream):
        total = own(stream, UP, 0)
        for direction in (DOWN, UP):
            turn = HOPS[stream, direction] - 1
            y_copies[stream, direction, turn].wait_recv()
            total = total + y_recv[stream, direction, turn].astype(F32)
        return total

    down_partial(0, 0)

    first_turn(0, DOWN)
    first_turn(1, UP)
    lax.fori_loop(1, 3, down_partial, 0)
    first_turn(0, UP)
    first_turn(1, DOWN)

    loads[2 + 2 * PARTS].wait()
    f_back[...] = jnp.dot(rct[...], wd[...], preferred_element_type=F32)

    def second_part(i, carry):
        rows = pl.ds(pl.multiple_of(i * 32, 32), 32)
        back = f_back[rows, :]
        d_hidden = back * factor_rows(rows)
        dpre[rows, 0:HID] = (d_hidden * f_gu[rows, 0:HID]).astype(BF)
        dpre[rows, HID : 2 * HID] = (d_hidden * f_gu[rows, HID : 2 * HID]).astype(BF)
        f_back[rows, :] = hid[rows, :].astype(F32) * back
        return carry

    lax.fori_loop(0, ROWS // 32, second_part, 0)

    dpre_copy = plain_copy(dpre, dpre_x, xs_sem.at[1], xr_sem.at[1], x_dev)
    second_half = (NY // 2) * (1 - core)
    lax.fori_loop(second_half, second_half + NY // 2, turn_rows, 0)
    def gu_partial(i, carry):
        t = dest(i)
        part = (
            jnp.dot(rows_t[t, half], dpre[...], preferred_element_type=F32)
            + jnp.dot(rows_x[t], dpre_x[...], preferred_element_type=F32)
        ).astype(BF)
        p_gu[t, 0] = part[:, 0:HID]
        p_gu[t, 1] = part[:, HID : 2 * HID]
        return carry

    def dx_part(q, carry):
        rows = pl.ds(pl.multiple_of(q * 8 * FEAT, 8 * FEAT), 8 * FEAT)
        part = dot_last(wgu[rows, :], dpre[...]).astype(BF)
        for m in range(8):
            dx_own[(m // 2) % 2, 4 * q + 2 * (m // 4) + m % 2] = part[m * FEAT : (m + 1) * FEAT]
        return carry

    lax.fori_loop(0, D // (8 * FEAT), dx_part, 0)
    folded = f_back[:, 0:128] + f_back[:, 128:256] + f_back[:, 256:384]
    dots = jnp.sum(folded.T, axis=0, keepdims=True)
    dt_own[...] = jnp.broadcast_to(dots, (8, ROWS))

    dx_core_copy = plain_copy(dx_own.at[lax.rem(xl + 1 + colour, 2)], dx_core, cs_sem.at[0], cr_sem.at[0], core_dev)
    dt_core_copy = plain_copy(dt_own, dt_core, cs_sem.at[1], cr_sem.at[1], core_dev)

    lax.fori_loop(3, NY, down_partial, 0)

    rows_copy.wait_recv()
    theirs = rows_x.at[mine]
    pass_copy = plain_copy(theirs, theirs, xs_sem.at[2], xr_sem.at[2], core_dev)

    for stream, direction in ((0, DOWN), (1, UP), (0, UP), (1, DOWN)):
        forward_turn(stream, direction, 1)

    def remote(src, dst, send, recv, device):
        return pltpu.make_async_remote_copy(
            src_ref=src, dst_ref=dst, send_sem=send, recv_sem=recv, device_id=device, device_id_type=MESH
        )

    def dx_xl_copy():
        return remote(dx_core, dx_xl, cs_sem.at[2], cr_sem.at[2], xl_dev)

    def dt_xl_copy():
        return remote(dt_sum, dt_xl, cs_sem.at[3], cr_sem.at[3], xl_dev)

    def z_copy(step):
        target = lax.rem(z + step, NZ)
        return remote(
            dx_core.at[pl.ds(2 * target, 2)], dx_z.at[step], zs_sem.at[0, step], zr_sem.at[0, step], z_dev(step)
        )

    def z_dot_copy(step):
        return remote(dt_z.at[0], dt_z.at[step], zs_sem.at[1, step], zr_sem.at[1, step], z_dev(step))

    def dx_out_copy():
        return remote(dx_out, dx_fin, cs_sem.at[4], cr_sem.at[4], core_dev)

    def dt_out_copy():
        return remote(dt_fin, dt_out, cs_sem.at[5], cr_sem.at[5], core_dev)

    dx_core_copy.wait_recv()
    dt_core_copy.wait_recv()
    dt_sum[...] = dt_own[...] + dt_core[...]

    @pl.when(colour == 1)
    def _():
        def add_core(i, carry):
            dx_core[i] = (dx_core[i].astype(F32) + dx_own[1 - xl, i].astype(F32)).astype(BF)
            return carry

        lax.fori_loop(0, 2 * NZ, add_core, 0)
        dx_xl_copy().start()
        dt_xl_copy().start()

    for stream, direction in ((0, DOWN), (1, UP), (0, UP), (1, DOWN)):
        forward_turn(stream, direction, 2)
    dpre_copy.wait_recv()
    pass_copy.wait_recv()
    gu_partial(0, 0)
    first_turn(2, DOWN)
    first_turn(3, UP)
    lax.fori_loop(1, 3, gu_partial, 0)
    first_turn(2, UP)
    first_turn(3, DOWN)
    @pl.when(colour == 0)
    def _():
        dx_xl_copy().wait_recv()
        dt_xl_copy().wait_recv()

        def add_four(i, carry):
            dx_core[i] = (
                dx_core[i].astype(F32) + dx_own[xl, i].astype(F32) + dx_xl[i].astype(F32)
            ).astype(BF)
            return carry

        lax.fori_loop(0, 2 * NZ, add_four, 0)
        dt_z[0] = dt_sum[...] + dt_xl[...]
        pl.semaphore_wait(barrier, NZ - 1)

        def z_start(step, carry):
            z_copy(step).start()
            z_dot_copy(step).start()
            return carry

        lax.fori_loop(1, NZ, z_start, 0)

    lax.fori_loop(3, NY, gu_partial, 0)


    forward_turn(0, DOWN, 3)
    forward_turn(1, UP, 3)
    for stream, direction in ((2, DOWN), (3, UP), (2, UP), (3, DOWN)):
        forward_turn(stream, direction, 1)

    ax_send[...] = last_sum(0).astype(BF)
    ax_copy = plain_copy(ax_send, ax_recv, as_sem.at[0], as_sem.at[1], x_dev)

    for stream, direction in ((2, DOWN), (3, UP), (2, UP), (3, DOWN)):
        forward_turn(stream, direction, 2)

    forward_turn(2, DOWN, 3)
    forward_turn(3, UP, 3)
    @pl.when(colour == 0)
    def _():
        def z_wait(step, carry):
            z_copy(step).wait_recv()
            z_dot_copy(step).wait_recv()
            return carry

        lax.fori_loop(1, NZ, z_wait, 0)

        def z_sum(step, total):
            return total + dx_z[step].astype(F32)

        dx_sum = lax.fori_loop(1, NZ, z_sum, dx_core[pl.ds(2 * z, 2)].astype(F32))
        f_back[0:FEAT, 0:ROWS] = dx_sum[0]
        f_back[FEAT : 2 * FEAT, 0:ROWS] = dx_sum[1]
        dx_out[...] = f_back[pl.ds(pl.multiple_of((1 - core) * FEAT, FEAT), FEAT), 0:ROWS].astype(BF)
        dx_fin[...] = f_back[pl.ds(pl.multiple_of(core * FEAT, FEAT), FEAT), 0:ROWS].astype(BF)
        dots = dt_z[z]
        for source in range(1, NZ):
            dots = dots + dt_z[lax.rem(z + NZ - source, NZ)]
        dt_fin[...] = dots
        dt_out[...] = dots
        dx_out_copy().start()
        dt_out_copy().start()

    down_sum = last_sum(1)
    ax_copy.wait_recv()
    gd_out[...] = (down_sum + ax_recv[...].astype(F32)).astype(BF)
    gg_out[...] = last_sum(2).astype(BF)
    gu_out[...] = last_sum(3).astype(BF)

    @pl.when(colour == 1)
    def _():
        dx_out_copy().wait_recv()
        dt_out_copy().wait_recv()

    grads = dx_fin[...].astype(F32)
    dots = dt_out[0:1, :]
    for j in range(3):
        block_cols = slice(j * BLOCK, (j + 1) * BLOCK)
        gtok_out[:, block_cols] = (
            grads[:, 0:BLOCK] * is_block[0][j] + grads[:, BLOCK:ROWS] * is_block[1][j]
        ).astype(BF)
        values = dots[:, 0:BLOCK] * (is_block[0][j] * live[0]) + dots[:, BLOCK:ROWS] * (is_block[1][j] * live[1])
        slots = slots_ref[:, block_cols]
        gprob_out[0:1, block_cols] = jnp.where(slots == 0, values, 0.0)
        gprob_out[1:2, block_cols] = jnp.where(slots == 1, values, 0.0)

    for copy in y_copies.values():
        copy.wait_send()
    for copy in (rows_copy, pass_copy, dpre_copy, dx_core_copy, dt_core_copy, ax_copy):
        copy.wait_send()

    @pl.when(colour == 1)
    def _():
        dx_xl_copy().wait_send()
        dt_xl_copy().wait_send()

    @pl.when(colour == 0)
    def _():
        def z_sent(step, carry):
            z_copy(step).wait_send()
            z_dot_copy(step).wait_send()
            return carry

        lax.fori_loop(1, NZ, z_sent, 0)
        dx_out_copy().wait_send()
        dt_out_copy().wait_send()


def body(tokens, cotangent, w_gate, w_up, w_down_t, gate_probs, slot_ids, block_list, block_count):
    smem = pl.BlockSpec(memory_space=pltpu.SMEM)
    vmem = pl.BlockSpec(memory_space=pltpu.VMEM)
    anywhere = pl.BlockSpec(memory_space=pl.ANY)
    dma = pltpu.SemaphoreType.DMA
    shard = (SHARD, HID)
    gtok, gprob, gg, gu, gd = pl.pallas_call(
        kernel,
        out_shape=(
            jax.ShapeDtypeStruct((FEAT, TOK), BF),
            jax.ShapeDtypeStruct((2, TOK), F32),
            jax.ShapeDtypeStruct(shard, BF),
            jax.ShapeDtypeStruct(shard, BF),
            jax.ShapeDtypeStruct(shard, BF),
        ),
        in_specs=[smem, smem, vmem, vmem] + [anywhere] * 5,
        out_specs=(vmem,) * 5,
        scratch_shapes=[
            pltpu.VMEM((TOK, D), BF),
            pltpu.VMEM((TOK, D), BF),
            pltpu.VMEM((D, 2 * HID), BF),
            pltpu.VMEM((D, HID), BF),
            pltpu.VMEM((ROWS, D), BF),
            pltpu.VMEM((ROWS, D), BF),
            pltpu.VMEM((ROWS, 2 * HID), F32),
            pltpu.VMEM((ROWS, HID), F32),
            pltpu.VMEM((ROWS, HID), BF),
            pltpu.VMEM((ROWS, HID), BF),
            pltpu.VMEM((ROWS, 2 * HID), BF),
            pltpu.VMEM((ROWS, BLOCK), F32),
            pltpu.VMEM((2, 3, 16, 128), BF),
            pltpu.VMEM((NY, 2, SHARD, ROWS), BF),
            pltpu.VMEM((NY, SHARD, ROWS), BF),
            pltpu.VMEM((ROWS, 2 * HID), BF),
            pltpu.VMEM((NY, 2) + shard, BF),
            pltpu.VMEM((NY, 2) + shard, BF),
            pltpu.VMEM((4, 2, 4) + shard, BF),
            pltpu.VMEM(shard, BF),
            pltpu.VMEM(shard, BF),
            pltpu.VMEM((2, 2 * NZ, FEAT, ROWS), BF),
            pltpu.VMEM((2 * NZ, FEAT, ROWS), BF),
            pltpu.VMEM((2 * NZ, FEAT, ROWS), BF),
            pltpu.VMEM((NZ, 2, FEAT, ROWS), BF),
            pltpu.VMEM((FEAT, ROWS), BF),
            pltpu.VMEM((FEAT, ROWS), BF),
            pltpu.VMEM((8, ROWS), F32),
            pltpu.VMEM((8, ROWS), F32),
            pltpu.VMEM((8, ROWS), F32),
            pltpu.VMEM((8, ROWS), F32),
            pltpu.VMEM((NZ, 8, ROWS), F32),
            pltpu.VMEM((8, ROWS), F32),
            pltpu.VMEM((8, ROWS), F32),
            dma((2 * PARTS + 3,)),
            dma((3,)),
            dma((3,)),
            dma((4, 2, 4)),
            dma((4, 2, 4)),
            dma((2,)),
            dma((6,)),
            dma((6,)),
            dma((2, NZ)),
            dma((2, NZ)),
            pltpu.SemaphoreType.REGULAR,
        ],
        compiler_params=pltpu.CompilerParams(
            collective_id=0, has_side_effects=True, vmem_limit_bytes=52 * 1024 * 1024
        ),
        name="expert_backward",
    )(
        block_list, block_count, gate_probs.T, slot_ids.reshape(1, TOK),
        tokens, cotangent, w_gate, w_up, w_down_t,
    )
    return gtok.T, gprob.T, gg, gu, gd


def solution(mesh):
    placed = (
        P("dp", None),
        P("dp", None),
        P(None, "blk"),
        P(None, "blk"),
        P(None, "blk"),
        P("dp", None),
        P("dp"),
        P("dp", None),
        P("dp"),
    )
    return jax.shard_map(
        body,
        mesh=mesh,
        in_specs=placed,
        out_specs=(P("dp", "blk"), P("dp", None), P("dp", "blk"), P("dp", "blk"), P("dp", "blk")),
        check_vma=False,
    )
```

```python
import jax
import jax.numpy as jnp
from jax import lax
from jax.experimental import pallas as pl
from jax.experimental.pallas import tpu as pltpu
from jax.sharding import PartitionSpec as P

MESH = pl.DeviceIdType.MESH
BF = jnp.bfloat16
F32 = jnp.float32

D = 3072
HID = 384
BLOCK = 128
TOK = 384
ROWS = 256
NY = 8
NZ = 12
SHARD = 192
FEAT = 64
CHUNK = 384
PARTS = 4

DOWN, UP = 0, 1
HOPS = {(0, DOWN): 4, (0, UP): 3, (1, DOWN): 3, (1, UP): 4, (2, DOWN): 4, (2, UP): 3, (3, DOWN): 3, (3, UP): 4}


def dot_lead(left, right):
    return lax.dot_general(left, right, (((0,), (0,)), ((), ())), preferred_element_type=F32)


def dot_last(left, right):
    return lax.dot_general(left, right, (((1,), (1,)), ((), ())), preferred_element_type=F32)


def kernel(
    list_ref, count_ref, probs_ref, slots_ref, tok_hbm, cot_hbm, wg_hbm, wu_hbm, wd_hbm,
    gtok_out, gprob_out, gg_out, gu_out, gd_out,
    tok, cot, wgu, wd, rin, rct, f_gu, f_back, hid, scaled, dpre, fac, picks,
    rows_t, rows_x, dpre_x, p_down, p_gu, y_recv, ax_send, ax_recv,
    dx_own, dx_core, dx_xl, dx_z, dx_out, dx_fin, dt_own, dt_core, dt_sum, dt_xl, dt_z, dt_out, dt_fin,
    load_sem, xs_sem, xr_sem, ys_sem, yr_sem, as_sem, cs_sem, cr_sem, zs_sem, zr_sem, ready,
):
    blk = lax.axis_index("blk")
    dp = lax.axis_index("dp")
    z = blk // 4
    xl = lax.rem(blk // 2, 2)
    core = lax.rem(blk, 2)
    y = dp // 2
    half = lax.rem(dp, 2)
    other = 1 - half
    colour = lax.rem(y + half + xl + core, 2)

    def at(zz=None, xx=None, cc=None):
        zz = z if zz is None else zz
        xx = xl if xx is None else xx
        cc = core if cc is None else cc
        return (zz * 4 + xx * 2 + cc, dp)

    y_dev = {
        DOWN: (blk, lax.rem(y + NY - 1, NY) * 2 + half),
        UP: (blk, lax.rem(y + 1, NY) * 2 + half),
    }
    x_dev = (blk, y * 2 + other)
    core_dev = at(cc=1 - core)
    xl_dev = at(xx=1 - xl)

    def z_dev(step):
        return at(zz=lax.rem(z + step, NZ))

    part_rows = D // PARTS
    sources = [(tok_hbm, tok), (cot_hbm, cot)]
    for k in range(PARTS):
        rows = pl.ds(k * part_rows, part_rows)
        sources.append((wg_hbm.at[rows], wgu.at[rows, 0:HID]))
        sources.append((wu_hbm.at[rows], wgu.at[rows, HID : 2 * HID]))
    sources.append((wd_hbm, wd))
    loads = [pltpu.make_async_copy(src, dst, load_sem.at[i]) for i, (src, dst) in enumerate(sources)]
    for load in loads:
        load.start()

    plane = (y_dev[DOWN], y_dev[UP], x_dev, core_dev, xl_dev)
    barrier = pltpu.get_barrier_semaphore()

    @pl.when(colour == 0)
    def _():
        for partner in plane:
            pl.semaphore_signal(barrier, inc=1, device_id=partner, device_id_type=MESH)
        for step in range(1, NZ):
            pl.semaphore_signal(barrier, inc=1, device_id=z_dev(step), device_id_type=MESH)

    blocks = [list_ref[0, k] for k in range(2)]
    live = [(count_ref[0] > k).astype(F32) for k in range(2)]
    is_block = [[(block == j).astype(F32) for j in range(3)] for block in blocks]

    gates_row = jnp.where(slots_ref[...] == 0, probs_ref[0:1, :], probs_ref[1:2, :])
    diagonal = lax.broadcasted_iota(jnp.int32, (BLOCK, BLOCK), 0) == lax.broadcasted_iota(
        jnp.int32, (BLOCK, BLOCK), 1
    )
    columns = [
        jnp.sum(jnp.where(diagonal, gates_row[:, j * BLOCK : (j + 1) * BLOCK], 0.0), axis=1, keepdims=True)
        for j in range(3)
    ]
    for k in range(2):
        column = sum(columns[j] * is_block[k][j] for j in range(3))
        fac[k * BLOCK : (k + 1) * BLOCK, :] = jnp.broadcast_to(column * live[k], (BLOCK, BLOCK))
        for j in range(3):
            picks[k, j] = jnp.broadcast_to(is_block[k][j], (16, 128)).astype(BF)

    def take_rows(source, target):
        def step(i, carry):
            for col in range(0, D, 128):
                parts = [source[pl.ds(pl.multiple_of(j * BLOCK + i * 16, 16), 16), col : col + 128] for j in range(3)]
                for k in range(2):
                    target[pl.ds(pl.multiple_of(k * BLOCK + i * 16, 16), 16), col : col + 128] = (
                        parts[0] * picks[k, 0] + parts[1] * picks[k, 1] + parts[2] * picks[k, 2]
                    )
            return carry

        lax.fori_loop(0, BLOCK // 16, step, 0)

    loads[0].wait()
    take_rows(tok, rin)

    @pl.when(colour == 1)
    def _():
        pl.semaphore_wait(barrier, len(plane))
        for partner in plane:
            pl.semaphore_signal(ready, inc=1, device_id=partner, device_id_type=MESH)

    def cols_of(t):
        return pl.ds(pl.multiple_of(t * CHUNK, CHUNK), CHUNK)

    def turn_rows(t, carry):
        part = rin[:, cols_of(t)].T
        rows_t[t, 0] = part[:SHARD]
        rows_t[t, 1] = part[SHARD:]
        return carry

    def plain_copy(src, dst, send, recv, device):
        copy = pltpu.make_async_remote_copy(
            src_ref=src, dst_ref=dst, send_sem=send, recv_sem=recv, device_id=device, device_id_type=MESH
        )
        copy.start()
        return copy

    first_half = (NY // 2) * core
    lax.fori_loop(first_half, first_half + NY // 2, turn_rows, 0)
    @pl.when(colour == 0)
    def _():
        pl.semaphore_wait(ready, len(plane))

    mine = pl.ds((NY // 2) * core, NY // 2)
    rows_copy = plain_copy(rows_t.at[mine, other], rows_x.at[mine], xs_sem.at[0], xr_sem.at[0], x_dev)

    loads[1].wait()
    take_rows(cot, rct)
    for k in range(PARTS):
        loads[2 + 2 * k].wait()
        loads[3 + 2 * k].wait()
        rows = slice(k * part_rows, (k + 1) * part_rows)
        product = jnp.dot(rin[:, rows], wgu[rows, :], preferred_element_type=F32)
        f_gu[...] = product if k == 0 else f_gu[...] + product

    def factor_rows(rows):
        column = fac[rows, :]
        return jnp.concatenate([column, column, column], axis=1)

    def first_part(i, carry):
        rows = pl.ds(pl.multiple_of(i * 32, 32), 32)
        pre_gate = f_gu[rows, 0:HID]
        pre_up = f_gu[rows, HID : 2 * HID]
        sig = jax.nn.sigmoid(pre_gate)
        act = pre_gate * sig
        hidden = (act * pre_up).astype(BF)
        hid[rows, :] = hidden
        scaled[rows, :] = (hidden.astype(F32) * factor_rows(rows)).astype(BF)
        f_gu[rows, 0:HID] = pre_up * sig * (1.0 + pre_gate * (1.0 - sig))
        f_gu[rows, HID : 2 * HID] = act
        return carry

    lax.fori_loop(0, ROWS // 32, first_part, 0)

    def dest(i):
        sign = 2 * (i % 2) - 1
        return lax.rem(y + 2 * NY + sign * (4 - (i + 1) // 2), NY)

    def order_of(direction, hop):
        if hop == 4:
            return 0
        return 7 - 2 * hop if direction == UP else 8 - 2 * hop

    def down_partial(i, carry):
        t = dest(i)
        part = dot_lead(rct[:, cols_of(t)], scaled[...]).astype(BF)
        p_down[t, 0] = part[:SHARD]
        p_down[t, 1] = part[SHARD:]
        return carry

    def y_copy(stream, direction, turn, src):
        return pltpu.make_async_remote_copy(
            src_ref=src,
            dst_ref=y_recv.at[stream, direction, turn],
            send_sem=ys_sem.at[stream, direction, turn],
            recv_sem=yr_sem.at[stream, direction, turn],
            device_id=y_dev[direction],
            device_id_type=MESH,
        )

    y_copies = {}

    def y_send(stream, direction, turn, src):
        copy = y_copy(stream, direction, turn, src)
        copy.start()
        y_copies[stream, direction, turn] = copy

    def own(stream, direction, hop):
        i = order_of(direction, hop)
        t = dest(i)
        if stream < 2:
            return p_down[t, other if stream == 0 else half].astype(F32)
        return p_gu[t, stream - 2].astype(F32)

    def first_turn(stream, direction):
        t = dest(order_of(direction, HOPS[stream, direction]))
        if stream < 2:
            y_send(stream, direction, 0, p_down.at[t, other if stream == 0 else half])
        else:
            y_send(stream, direction, 0, p_gu.at[t, stream - 2])

    def forward_turn(stream, direction, turn):
        y_copies[stream, direction, turn - 1].wait_recv()
        slot = y_recv.at[stream, direction, turn - 1]
        slot[...] = (slot[...].astype(F32) + own(stream, direction, HOPS[stream, direction] - turn)).astype(BF)
        y_send(stream, direction, turn, slot)

    def last_sum(stream):
        total = own(stream, UP, 0)
        for direction in (DOWN, UP):
            turn = HOPS[stream, direction] - 1
            y_copies[stream, direction, turn].wait_recv()
            total = total + y_recv[stream, direction, turn].astype(F32)
        return total

    down_partial(0, 0)

    first_turn(0, DOWN)
    first_turn(1, UP)

    loads[2 + 2 * PARTS].wait()
    f_back[...] = jnp.dot(rct[...], wd[...], preferred_element_type=F32)

    def second_part(i, carry):
        rows = pl.ds(pl.multiple_of(i * 32, 32), 32)
        back = f_back[rows, :]
        d_hidden = back * factor_rows(rows)
        dpre[rows, 0:HID] = (d_hidden * f_gu[rows, 0:HID]).astype(BF)
        dpre[rows, HID : 2 * HID] = (d_hidden * f_gu[rows, HID : 2 * HID]).astype(BF)
        f_back[rows, :] = hid[rows, :].astype(F32) * back
        return carry

    lax.fori_loop(0, ROWS // 32, second_part, 0)

    dpre_copy = plain_copy(dpre, dpre_x, xs_sem.at[1], xr_sem.at[1], x_dev)
    lax.fori_loop(1, 3, down_partial, 0)
    first_turn(0, UP)
    first_turn(1, DOWN)
    second_half = (NY // 2) * (1 - core)
    lax.fori_loop(second_half, second_half + NY // 2, turn_rows, 0)
    def gu_partial(i, carry):
        t = dest(i)
        part = (
            jnp.dot(rows_t[t, half], dpre[...], preferred_element_type=F32)
            + jnp.dot(rows_x[t], dpre_x[...], preferred_element_type=F32)
        ).astype(BF)
        p_gu[t, 0] = part[:, 0:HID]
        p_gu[t, 1] = part[:, HID : 2 * HID]
        return carry

    def dx_part(q, carry):
        rows = pl.ds(pl.multiple_of(q * 8 * FEAT, 8 * FEAT), 8 * FEAT)
        part = dot_last(wgu[rows, :], dpre[...]).astype(BF)
        for m in range(8):
            dx_own[(m // 2) % 2, 4 * q + 2 * (m // 4) + m % 2] = part[m * FEAT : (m + 1) * FEAT]
        return carry

    lax.fori_loop(0, D // (8 * FEAT), dx_part, 0)
    folded = f_back[:, 0:128] + f_back[:, 128:256] + f_back[:, 256:384]
    dots = jnp.sum(folded.T, axis=0, keepdims=True)
    dt_own[...] = jnp.broadcast_to(dots, (8, ROWS))

    dx_core_copy = plain_copy(dx_own.at[lax.rem(xl + 1 + colour, 2)], dx_core, cs_sem.at[0], cr_sem.at[0], core_dev)
    dt_core_copy = plain_copy(dt_own, dt_core, cs_sem.at[1], cr_sem.at[1], core_dev)

    lax.fori_loop(3, NY, down_partial, 0)

    rows_copy.wait_recv()
    theirs = rows_x.at[mine]
    pass_copy = plain_copy(theirs, theirs, xs_sem.at[2], xr_sem.at[2], core_dev)

    for stream, direction in ((0, DOWN), (1, UP), (0, UP), (1, DOWN)):
        forward_turn(stream, direction, 1)

    def remote(src, dst, send, recv, device):
        return pltpu.make_async_remote_copy(
            src_ref=src, dst_ref=dst, send_sem=send, recv_sem=recv, device_id=device, device_id_type=MESH
        )

    def dx_xl_copy():
        return remote(dx_core, dx_xl, cs_sem.at[2], cr_sem.at[2], xl_dev)

    def dt_xl_copy():
        return remote(dt_sum, dt_xl, cs_sem.at[3], cr_sem.at[3], xl_dev)

    def z_copy(step):
        target = lax.rem(z + step, NZ)
        return remote(
            dx_core.at[pl.ds(2 * target, 2)], dx_z.at[step], zs_sem.at[0, step], zr_sem.at[0, step], z_dev(step)
        )

    def z_dot_copy(step):
        return remote(dt_z.at[0], dt_z.at[step], zs_sem.at[1, step], zr_sem.at[1, step], z_dev(step))

    def dx_out_copy():
        return remote(dx_out, dx_fin, cs_sem.at[4], cr_sem.at[4], core_dev)

    def dt_out_copy():
        return remote(dt_fin, dt_out, cs_sem.at[5], cr_sem.at[5], core_dev)

    dx_core_copy.wait_recv()
    dt_core_copy.wait_recv()
    dt_sum[...] = dt_own[...] + dt_core[...]

    @pl.when(colour == 1)
    def _():
        def add_core(i, carry):
            dx_core[i] = (dx_core[i].astype(F32) + dx_own[1 - xl, i].astype(F32)).astype(BF)
            return carry

        lax.fori_loop(0, 2 * NZ, add_core, 0)
        dx_xl_copy().start()
        dt_xl_copy().start()

    for stream, direction in ((0, DOWN), (1, UP), (0, UP), (1, DOWN)):
        forward_turn(stream, direction, 2)
    dpre_copy.wait_recv()
    pass_copy.wait_recv()
    gu_partial(0, 0)
    first_turn(2, DOWN)
    first_turn(3, UP)
    lax.fori_loop(1, 3, gu_partial, 0)
    first_turn(2, UP)
    first_turn(3, DOWN)
    @pl.when(colour == 0)
    def _():
        dx_xl_copy().wait_recv()
        dt_xl_copy().wait_recv()

        def add_four(i, carry):
            dx_core[i] = (
                dx_core[i].astype(F32) + dx_own[xl, i].astype(F32) + dx_xl[i].astype(F32)
            ).astype(BF)
            return carry

        lax.fori_loop(0, 2 * NZ, add_four, 0)
        dt_z[0] = dt_sum[...] + dt_xl[...]
        pl.semaphore_wait(barrier, NZ - 1)

        def z_start(step, carry):
            z_copy(step).start()
            z_dot_copy(step).start()
            return carry

        lax.fori_loop(1, NZ, z_start, 0)

    lax.fori_loop(3, NY, gu_partial, 0)


    forward_turn(0, DOWN, 3)
    forward_turn(1, UP, 3)
    for stream, direction in ((2, DOWN), (3, UP), (2, UP), (3, DOWN)):
        forward_turn(stream, direction, 1)

    ax_send[...] = last_sum(0).astype(BF)
    ax_copy = plain_copy(ax_send, ax_recv, as_sem.at[0], as_sem.at[1], x_dev)

    for stream, direction in ((2, DOWN), (3, UP), (2, UP), (3, DOWN)):
        forward_turn(stream, direction, 2)

    forward_turn(2, DOWN, 3)
    forward_turn(3, UP, 3)
    @pl.when(colour == 0)
    def _():
        def z_wait(step, carry):
            z_copy(step).wait_recv()
            z_dot_copy(step).wait_recv()
            return carry

        lax.fori_loop(1, NZ, z_wait, 0)

        def z_sum(step, total):
            return total + dx_z[step].astype(F32)

        dx_sum = lax.fori_loop(1, NZ, z_sum, dx_core[pl.ds(2 * z, 2)].astype(F32))
        f_back[0:FEAT, 0:ROWS] = dx_sum[0]
        f_back[FEAT : 2 * FEAT, 0:ROWS] = dx_sum[1]
        dx_out[...] = f_back[pl.ds(pl.multiple_of((1 - core) * FEAT, FEAT), FEAT), 0:ROWS].astype(BF)
        dx_fin[...] = f_back[pl.ds(pl.multiple_of(core * FEAT, FEAT), FEAT), 0:ROWS].astype(BF)
        dots = dt_z[z]
        for source in range(1, NZ):
            dots = dots + dt_z[lax.rem(z + NZ - source, NZ)]
        dt_fin[...] = dots
        dt_out[...] = dots
        dx_out_copy().start()
        dt_out_copy().start()

    down_sum = last_sum(1)
    ax_copy.wait_recv()
    gd_out[...] = (down_sum + ax_recv[...].astype(F32)).astype(BF)
    gg_out[...] = last_sum(2).astype(BF)
    gu_out[...] = last_sum(3).astype(BF)

    @pl.when(colour == 1)
    def _():
        dx_out_copy().wait_recv()
        dt_out_copy().wait_recv()

    grads = dx_fin[...].astype(F32)
    dots = dt_out[0:1, :]
    for j in range(3):
        block_cols = slice(j * BLOCK, (j + 1) * BLOCK)
        gtok_out[:, block_cols] = (
            grads[:, 0:BLOCK] * is_block[0][j] + grads[:, BLOCK:ROWS] * is_block[1][j]
        ).astype(BF)
        values = dots[:, 0:BLOCK] * (is_block[0][j] * live[0]) + dots[:, BLOCK:ROWS] * (is_block[1][j] * live[1])
        slots = slots_ref[:, block_cols]
        gprob_out[0:1, block_cols] = jnp.where(slots == 0, values, 0.0)
        gprob_out[1:2, block_cols] = jnp.where(slots == 1, values, 0.0)

    for copy in y_copies.values():
        copy.wait_send()
    for copy in (rows_copy, pass_copy, dpre_copy, dx_core_copy, dt_core_copy, ax_copy):
        copy.wait_send()

    @pl.when(colour == 1)
    def _():
        dx_xl_copy().wait_send()
        dt_xl_copy().wait_send()

    @pl.when(colour == 0)
    def _():
        def z_sent(step, carry):
            z_copy(step).wait_send()
            z_dot_copy(step).wait_send()
            return carry

        lax.fori_loop(1, NZ, z_sent, 0)
        dx_out_copy().wait_send()
        dt_out_copy().wait_send()


def body(tokens, cotangent, w_gate, w_up, w_down_t, gate_probs, slot_ids, block_list, block_count):
    smem = pl.BlockSpec(memory_space=pltpu.SMEM)
    vmem = pl.BlockSpec(memory_space=pltpu.VMEM)
    anywhere = pl.BlockSpec(memory_space=pl.ANY)
    dma = pltpu.SemaphoreType.DMA
    shard = (SHARD, HID)
    gtok, gprob, gg, gu, gd = pl.pallas_call(
        kernel,
        out_shape=(
            jax.ShapeDtypeStruct((FEAT, TOK), BF),
            jax.ShapeDtypeStruct((2, TOK), F32),
            jax.ShapeDtypeStruct(shard, BF),
            jax.ShapeDtypeStruct(shard, BF),
            jax.ShapeDtypeStruct(shard, BF),
        ),
        in_specs=[smem, smem, vmem, vmem] + [anywhere] * 5,
        out_specs=(vmem,) * 5,
        scratch_shapes=[
            pltpu.VMEM((TOK, D), BF),
            pltpu.VMEM((TOK, D), BF),
            pltpu.VMEM((D, 2 * HID), BF),
            pltpu.VMEM((D, HID), BF),
            pltpu.VMEM((ROWS, D), BF),
            pltpu.VMEM((ROWS, D), BF),
            pltpu.VMEM((ROWS, 2 * HID), F32),
            pltpu.VMEM((ROWS, HID), F32),
            pltpu.VMEM((ROWS, HID), BF),
            pltpu.VMEM((ROWS, HID), BF),
            pltpu.VMEM((ROWS, 2 * HID), BF),
            pltpu.VMEM((ROWS, BLOCK), F32),
            pltpu.VMEM((2, 3, 16, 128), BF),
            pltpu.VMEM((NY, 2, SHARD, ROWS), BF),
            pltpu.VMEM((NY, SHARD, ROWS), BF),
            pltpu.VMEM((ROWS, 2 * HID), BF),
            pltpu.VMEM((NY, 2) + shard, BF),
            pltpu.VMEM((NY, 2) + shard, BF),
            pltpu.VMEM((4, 2, 4) + shard, BF),
            pltpu.VMEM(shard, BF),
            pltpu.VMEM(shard, BF),
            pltpu.VMEM((2, 2 * NZ, FEAT, ROWS), BF),
            pltpu.VMEM((2 * NZ, FEAT, ROWS), BF),
            pltpu.VMEM((2 * NZ, FEAT, ROWS), BF),
            pltpu.VMEM((NZ, 2, FEAT, ROWS), BF),
            pltpu.VMEM((FEAT, ROWS), BF),
            pltpu.VMEM((FEAT, ROWS), BF),
            pltpu.VMEM((8, ROWS), F32),
            pltpu.VMEM((8, ROWS), F32),
            pltpu.VMEM((8, ROWS), F32),
            pltpu.VMEM((8, ROWS), F32),
            pltpu.VMEM((NZ, 8, ROWS), F32),
            pltpu.VMEM((8, ROWS), F32),
            pltpu.VMEM((8, ROWS), F32),
            dma((2 * PARTS + 3,)),
            dma((3,)),
            dma((3,)),
            dma((4, 2, 4)),
            dma((4, 2, 4)),
            dma((2,)),
            dma((6,)),
            dma((6,)),
            dma((2, NZ)),
            dma((2, NZ)),
            pltpu.SemaphoreType.REGULAR,
        ],
        compiler_params=pltpu.CompilerParams(
            collective_id=0, has_side_effects=True, vmem_limit_bytes=52 * 1024 * 1024
        ),
        name="expert_backward",
    )(
        block_list, block_count, gate_probs.T, slot_ids.reshape(1, TOK),
        tokens, cotangent, w_gate, w_up, w_down_t,
    )
    return gtok.T, gprob.T, gg, gu, gd


def solution(mesh):
    placed = (
        P("dp", None),
        P("dp", None),
        P(None, "blk"),
        P(None, "blk"),
        P(None, "blk"),
        P("dp", None),
        P("dp"),
        P("dp", None),
        P("dp"),
    )
    return jax.shard_map(
        body,
        mesh=mesh,
        in_specs=placed,
        out_specs=(P("dp", "blk"), P("dp", None), P("dp", "blk"), P("dp", "blk"), P("dp", "blk")),
        check_vma=False,
    )
```
